256 devices in a mesh: stn: 32 (over y, z_hi, core), tm: 8 (over z_lo, x).
Axes of the slice: x: 4, y: 4, z: 8 (z_hi: 4, z_lo: 2; z = z_hi * 2 + z_lo), core: 2. Of those that a mesh axis runs over, the one named last changes fastest.
Arguments:
- voltages: int32 [512, 2, 131072], P('stn', None, 'tm'), may hold values from -127 to 127
- filter_taps: float32 [16, 1024], replicated, may hold values from -1.5 to 1.5
- reference_channel: int32 [1], replicated, may hold values from 0 to 511
- basis_inputs: int32 [8], replicated, may hold values from 0 to 511, as said below
Outputs:
- covariance: bfloat16 [512, 512, 1024], P(('stn', 'tm'))
- projection: float32 [512, 128], P(('stn', 'tm'))
- subspace_power: float32 [512, 128], P('stn', 'tm')
The draws below stay inside these ranges and needn't reach their ends.
Inputs may be any that keep to these rules, and one draw needn't show every extreme that they name: `basis_inputs`: 8 distinct input indices.
All inputs are finite; a program needn't handle non-finite values.
Results may differ from the reference program's by a relative error of at most 0.012.
Values may be sent and summed in bfloat16 or wider, within the bound.
A program may use at most 64 MiB of HBM per device.

```python
import math
import jax
import jax.numpy as jnp
from jax import lax

INPUTS = 512
NFFT = 1024
FCH = 512
TAPS = 16
K = 8
T_DEV = 16
SPECTRA = 128
SAMPLES = 131072
N_TM = 8


def draw_voltages(key, part):
    level_key, noise_key, gain_key, tone_key = jax.random.split(key, 4)
    levels = jnp.array([12, 16, 24, 32, 48, 64, 80, 95], dtype=jnp.int32)
    level_index = jax.random.randint(level_key, (INPUTS,), 0, 8, dtype=jnp.int32)
    amplitude = levels[level_index][:, None, None]
    noise = jax.random.randint(noise_key, (INPUTS, 2, SAMPLES), -amplitude, amplitude + 1, dtype=jnp.int32)
    gain = jax.random.randint(gain_key, (INPUTS, 1, 1), -4, 5, dtype=jnp.int32)
    interferer = jax.random.randint(tone_key, (1, 2, SAMPLES), -8, 9, dtype=jnp.int32)
    return (noise + gain * interferer).astype(jnp.int32)


def draw_basis_inputs(key, part):
    order = jax.random.permutation(key, INPUTS)
    return order[:K].astype(jnp.int32)


def gaussian(own_key, dims, scale, reach, kind=jnp.bfloat16):
    drawn = scale * jax.random.normal(own_key, dims, jnp.float32)
    return jnp.clip(drawn, min=-reach, max=reach).astype(kind)


def setup_inputs(seed: int = 0) -> dict:
    streams_of = jax.random.split(jax.random.key(seed), 5)
    voltages = draw_voltages(jax.random.fold_in(streams_of[4], 71), 0)
    filter_taps = gaussian(streams_of[1], (TAPS, NFFT), TAPS ** -0.5, 1.5, jnp.float32)
    reference_channel = jax.random.randint(streams_of[2], (1,), 0, FCH).astype(jnp.int32)
    basis_inputs = draw_basis_inputs(jax.random.fold_in(streams_of[4], 71), 0)
    return {"voltages": voltages, "filter_taps": filter_taps, "reference_channel": reference_channel, "basis_inputs": basis_inputs}


def transform_tables():
    sample = jnp.arange(NFFT, dtype=jnp.int32)
    channel = jnp.arange(FCH, dtype=jnp.int32)
    phase = sample[:, None] * channel[None, :] % NFFT
    angle = phase.astype(jnp.float32) * (2.0 * math.pi / NFFT)
    factor = 1.0 / math.sqrt(NFFT)
    cosine = jnp.cos(angle) * factor
    sine = jnp.sin(angle) * factor
    table_re = jnp.stack([cosine, -sine], axis=2).reshape(NFFT, 2 * FCH).astype(jnp.bfloat16)
    table_im = jnp.stack([sine, cosine], axis=2).reshape(NFFT, 2 * FCH).astype(jnp.bfloat16)
    return (table_re, table_im)

def orthonormal(col_real, col_imag):
    basis_real = []
    basis_imag = []
    for column in range(col_real.shape[1]):
        vec_real = col_real[:, column]
        vec_imag = col_imag[:, column]
        for former in range(column):
            q_real = basis_real[former]
            q_imag = basis_imag[former]
            inner_real = jnp.sum(q_real * vec_real + q_imag * vec_imag)
            inner_imag = jnp.sum(q_real * vec_imag - q_imag * vec_real)
            vec_real = vec_real - (q_real * inner_real - q_imag * inner_imag)
            vec_imag = vec_imag - (q_real * inner_imag + q_imag * inner_real)
        inverse = lax.rsqrt(jnp.sum(vec_real * vec_real + vec_imag * vec_imag) + 1e-06)
        basis_real.append(vec_real * inverse)
        basis_imag.append(vec_imag * inverse)
    return (jnp.stack(basis_real, axis=1), jnp.stack(basis_imag, axis=1))

def reference(voltages, filter_taps, reference_channel, basis_inputs):
    table_re, table_im = transform_tables()

    def channelize(single):
        frames = (single.astype(jnp.float32) / 64.0).reshape(2, SPECTRA, NFFT)
        padded = jnp.pad(frames, ((0, 0), (TAPS - 1, 0), (0, 0)))
        accum = jnp.zeros((2, SPECTRA, NFFT), jnp.float32)
        for tap_index in range(TAPS):
            accum = accum + filter_taps[tap_index] * padded[:, tap_index:tap_index + SPECTRA, :]
        filtered = accum.astype(jnp.bfloat16)
        result = jnp.dot(filtered[0], table_re, preferred_element_type=jnp.float32)
        result = result + jnp.dot(filtered[1], table_im, preferred_element_type=jnp.float32)
        return result.astype(jnp.bfloat16)
    spectra = lax.map(channelize, voltages)

    def channel_data(index):
        piece = lax.dynamic_slice_in_dim(spectra, (2 * index).astype(jnp.int32), 2, 2)
        return (piece[:, :, 0].astype(jnp.float32), piece[:, :, 1].astype(jnp.float32))

    def averaged_cov(chan_real, chan_imag):
        block_real = chan_real.reshape(INPUTS, N_TM, T_DEV)
        block_imag = chan_imag.reshape(INPUTS, N_TM, T_DEV)
        sum_real = jnp.einsum('imt,jmt->mij', block_real, block_real) + jnp.einsum('imt,jmt->mij', block_imag, block_imag)
        sum_imag = jnp.einsum('imt,jmt->mij', block_imag, block_real) - jnp.einsum('imt,jmt->mij', block_real, block_imag)
        terms = jnp.concatenate([sum_real, sum_imag], axis=2)
        rounded = lax.optimization_barrier(terms.astype(jnp.bfloat16)).astype(jnp.float32)
        return lax.optimization_barrier(jnp.sum(rounded, axis=0)) / SPECTRA
    ref_real, ref_imag = channel_data(reference_channel[0])
    ref_cov = averaged_cov(ref_real, ref_imag)
    col_real = ref_cov[:, :INPUTS][:, basis_inputs]
    col_imag = ref_cov[:, INPUTS:][:, basis_inputs]
    basis_real, basis_imag = orthonormal(col_real, col_imag)
    low_real = lax.optimization_barrier(basis_real.astype(jnp.bfloat16)).astype(jnp.float32)
    low_imag = lax.optimization_barrier(basis_imag.astype(jnp.bfloat16)).astype(jnp.float32)
    highest = lax.Precision.HIGHEST

    def per_channel(index):
        chan_real, chan_imag = channel_data(index)
        averaged = averaged_cov(chan_real, chan_imag)
        cov_real = averaged[:, :INPUTS]
        cov_imag = averaged[:, INPUTS:]
        prod_real = jnp.dot(cov_real, basis_real, precision=highest) - jnp.dot(cov_imag, basis_imag, precision=highest)
        prod_imag = jnp.dot(cov_real, basis_imag, precision=highest) + jnp.dot(cov_imag, basis_real, precision=highest)
        proj_real = jnp.dot(basis_real.T, prod_real, precision=highest) + jnp.dot(basis_imag.T, prod_imag, precision=highest)
        proj_imag = jnp.dot(basis_real.T, prod_imag, precision=highest) - jnp.dot(basis_imag.T, prod_real, precision=highest)
        projection = jnp.concatenate([proj_real.reshape(-1), proj_imag.reshape(-1)])
        sub_real = jnp.dot(low_real.T, chan_real, precision=highest) + jnp.dot(low_imag.T, chan_imag, precision=highest)
        sub_imag = jnp.dot(low_real.T, chan_imag, precision=highest) - jnp.dot(low_imag.T, chan_real, precision=highest)
        power = lax.optimization_barrier(jnp.sum(sub_real * sub_real + sub_imag * sub_imag, axis=0))
        return (averaged.astype(jnp.bfloat16), projection, power)
    covariance, projection, power = lax.map(per_channel, jnp.arange(FCH, dtype=jnp.int32))
    return (covariance, projection, power)
```

```python
import functools
import math

import jax
import jax.numpy as jnp
import numpy as np
from jax import lax
from jax.experimental import pallas as pl
from jax.experimental.pallas import tpu as pltpu
from jax.sharding import PartitionSpec as P

NFFT = 1024
FCH = 512
TAPS = 16
K = 8
INPUTS = 512
SPECTRA = 128
STN = 32
TM = 8
LOCAL = INPUTS // STN
FRAMES = SPECTRA // TM
SUB = NFFT // 128
Q = 2 * SUB
SPILL = TAPS - 1
TILES = 4
CH = 1
NCH = TILES // CH
WIDE = CH * 128
MESH = pl.DeviceIdType.MESH
F32 = jnp.float32
BF16 = jnp.bfloat16
HIGHEST = lax.Precision.HIGHEST


def transform_table():
    phase = np.arange(NFFT)[:, None] * np.arange(FCH)[None, :] % NFFT
    angle = phase.astype(np.float32) * np.float32(2.0 * math.pi / NFFT)
    factor = np.float32(1.0 / math.sqrt(NFFT))
    cosine, sine = np.cos(angle) * factor, np.sin(angle) * factor
    table_re = np.stack([cosine, -sine], axis=2)
    table_im = np.stack([sine, cosine], axis=2)
    both = np.stack([table_re.reshape(SUB, 128, FCH, 2), table_im.reshape(SUB, 128, FCH, 2)], axis=1)
    both = both.reshape(2 * NFFT, 2, 16, TILES, 2, 2, 2)
    both = both.transpose(3, 0, 1, 4, 2, 5, 6)
    both = both.reshape(NCH, CH, 2 * NFFT, 256).transpose(0, 2, 1, 3)
    return both.reshape(NCH, 2 * NFFT, 2 * WIDE).astype(jnp.bfloat16)


def butterfly(blocks, lane):
    blocks = list(blocks)
    for bit in range(4):
        step, shift = 1 << bit, 4 << bit
        low = (lane & shift) == 0
        for a in range(16):
            if a & step:
                continue
            first, second = blocks[a], blocks[a | step]
            blocks[a] = jnp.where(low, first, pltpu.roll(second, shift, 1))
            blocks[a | step] = jnp.where(low, pltpu.roll(first, 128 - shift, 1), second)
    return blocks


def gram_schmidt(vec_re, vec_im):
    row = lax.broadcasted_iota(jnp.int32, (K, 1), 0)
    for k in range(K):
        w_re, w_im = vec_re[k : k + 1], vec_im[k : k + 1]
        in_re = jnp.sum(w_re * vec_re + w_im * vec_im, axis=1, keepdims=True)
        in_im = jnp.sum(w_re * vec_im - w_im * vec_re, axis=1, keepdims=True)
        inverse = lax.rsqrt(in_re[k : k + 1] + 1e-06)
        q_re, q_im = w_re * inverse, w_im * inverse
        c_re = jnp.where(row > k, in_re * inverse, 0.0)
        c_im = jnp.where(row > k, in_im * inverse, 0.0)
        new_re = vec_re - (q_re * c_re - q_im * c_im)
        new_im = vec_im - (q_re * c_im + q_im * c_re)
        vec_re = jnp.where(row == k, q_re, new_re)
        vec_im = jnp.where(row == k, q_im, new_im)
    return vec_re, vec_im


def channelise_kernel(
    volt, taps, table_hbm, ref_chan, basis_in,
    u, v, basis,
    table, tap_rows, frames_f, lhs, halo_out, halo_in, send1, send2, cols_out, cols_a, cols_b, cols_c,
    table_sem, halo_ss, halo_rs, ss1, rs1, ss2, rs2, css, crs_a, crs_b, crs_c,
):
    s = lax.axis_index("stn")
    t = lax.axis_index("tm")
    barrier = pltpu.get_barrier_semaphore()

    @pl.loop(1, STN)
    def _(d):
        pl.semaphore_signal(barrier, 1, device_id={"stn": lax.rem(s + d, STN)}, device_id_type=MESH)

    @pl.loop(1, TM)
    def _(d):
        pl.semaphore_signal(barrier, 1, device_id={"tm": lax.rem(t + d, TM)}, device_id_type=MESH)

    load_table = pltpu.make_async_copy(table_hbm, table, table_sem)
    load_table.start()

    for sub in range(SUB):
        part = taps[:, sub * 128 : (sub + 1) * 128] * (1.0 / 64.0)
        for p in range(2):
            tap_rows[pl.ds(sub * 2 + p, TAPS, stride=Q), :] = part

    def filter_frames(spill):
        @pl.loop(0, LOCAL * 2)
        def _(step):
            i, half = step // 2, lax.rem(step, 2)
            base = pl.multiple_of(i * (FRAMES * Q) + half * 8, 8)
            x = [volt[pl.ds(base + f * Q, 8), :].astype(F32) for f in range(FRAMES)]
            tap = [tap_rows[pl.ds(pl.multiple_of(k * Q + half * 8, 8), 8), :] for k in range(TAPS)]
            for f in range(SPILL if spill else FRAMES):
                acc = None
                for j in range(f + 1, FRAMES) if spill else range(f + 1):
                    k = j - f - 1 if spill else SPILL - f + j
                    term = tap[k] * x[j]
                    acc = term if acc is None else acc + term
                row = pl.multiple_of((f * LOCAL + i) * Q + half * 8, 8)
                frames_f[pl.ds(row, 8), :] = acc

        rows = (SPILL if spill else FRAMES) * LOCAL
        for q in range(Q):
            lhs[0:rows, q * 128 : (q + 1) * 128] = frames_f[pl.ds(q, rows, stride=Q), :].astype(BF16)

    def chunk_of(block, step):
        return lax.rem(block // (2 * CH) + 1 + step, NCH)

    def halo_copy(j):
        return pltpu.make_async_remote_copy(
            src_ref=halo_out.at[j],
            dst_ref=halo_in.at[j],
            send_sem=halo_ss.at[j],
            recv_sem=halo_rs.at[j],
            device_id={"tm": lax.rem(t + 1, TM)},
            device_id_type=MESH,
        )

    def stage1_copy(j, to):
        return pltpu.make_async_remote_copy(
            src_ref=send1.at[j, pl.ds(pl.multiple_of(to * LOCAL, LOCAL), LOCAL)],
            dst_ref=u.at[j, pl.ds(pl.multiple_of(s * LOCAL, LOCAL), LOCAL)],
            send_sem=ss1.at[j],
            recv_sem=rs1.at[j],
            device_id={"stn": to},
            device_id_type=MESH,
        )

    def stage2_copy(to):
        return pltpu.make_async_remote_copy(
            src_ref=send2.at[to],
            dst_ref=v.at[t],
            send_sem=ss2.at[to],
            recv_sem=rs2.at[t],
            device_id={"tm": to},
            device_id_type=MESH,
        )

    def bytes_of(ref, sem):
        pltpu.make_async_copy(ref, ref, sem).wait()

    filter_frames(True)
    load_table.wait()
    pl.semaphore_wait(barrier, STN - 1 + TM - 1)
    for step in range(NCH):
        j = chunk_of(lax.rem(t + 1, TM), step)
        part = jnp.dot(lhs[0 : SPILL * LOCAL, :], table[j], preferred_element_type=F32)
        halo_out[j] = part.astype(BF16)

        @pl.when(t < TM - 1)
        def _():
            halo_copy(j).start()

    filter_frames(False)

    @pl.when(t == 0)
    def _():
        halo_in[...] = jnp.zeros_like(halo_in)

    lane = lax.broadcasted_iota(jnp.int32, (1, 128), 1)

    def stage1(step):
        j = chunk_of(t, step)
        own = jnp.dot(lhs[...], table[j], preferred_element_type=F32)

        @pl.when(t > 0)
        def _():
            bytes_of(halo_in.at[j], halo_rs.at[j])

        head = own[0 : SPILL * LOCAL] + halo_in[j].astype(F32)
        own = jnp.concatenate([head, own[SPILL * LOCAL :]], axis=0)
        own = own.astype(BF16).astype(F32)
        for c in range(CH):
            for hi in range(2):
                at = (c * 2 + hi) * 128
                blocks = [own[f * LOCAL : (f + 1) * LOCAL, at : at + 128] for f in range(FRAMES)]
                for g, block in enumerate(butterfly(blocks, lane)):
                    row = (hi * 16 + g) * LOCAL
                    send1[j, row : row + LOCAL, c * 128 : (c + 1) * 128] = block.astype(BF16)
        mine = pl.ds(pl.multiple_of(s * LOCAL, LOCAL), LOCAL)
        u[j, mine, :] = send1[j, mine, :]

        @pl.loop(1, STN)
        def _(d):
            stage1_copy(j, lax.rem(s + d, STN)).start()

    def stage2(step):
        j = chunk_of(t, step)
        bytes_of(u.at[j, pl.ds(0, INPUTS - LOCAL)], rs1.at[j])
        for c in range(CH):
            block = u[j, :, c * 128 : (c + 1) * 128].astype(F32)
            low, high = block[0 : INPUTS // 2], block[INPUTS // 2 :]
            first = lane < 64
            pair = (
                jnp.where(first, low, pltpu.roll(high, 64, 1)),
                jnp.where(first, pltpu.roll(low, 64, 1), high),
            )
            for b in range(2):
                to = (j * CH + c) * 2 + b
                send2[to] = pair[b].astype(BF16)

                @pl.when(to != t)
                def _():
                    stage2_copy(to).start()

    stage1(0)
    for step in range(1, NCH):
        stage1(step)
        stage2(step - 1)
    stage2(NCH - 1)
    v[t] = send2[t]

    ref = ref_chan[0]
    ref_stn, ref_tm, ref_low = ref // 16, lax.rem(ref // 2, TM), lax.rem(ref, 2)
    row16 = lax.broadcasted_iota(jnp.int32, (2 * K, 1), 0)
    wanted = jnp.zeros((2 * K, 1), jnp.int32)
    for k in range(K):
        wanted = jnp.where(lax.rem(row16, K) == k, basis_in[k], wanted)
    column = lax.broadcasted_iota(jnp.int32, (2 * K, INPUTS), 1)
    onehot = jnp.where(column == wanted, 1.0, 0.0).astype(BF16)
    columns = jnp.zeros((2 * K, INPUTS), F32)
    here = jnp.where(s == ref_stn, 1, 0)
    for q in range(TILES):
        block = u[q // CH, :, (q % CH) * 128 : (q % CH + 1) * 128]
        picked = jnp.dot(onehot, block, preferred_element_type=F32)
        swapped = jnp.where((lane & 1) == 0, -pltpu.roll(picked, 127, 1), pltpu.roll(picked, 1, 1))
        left = jnp.where(row16 < K, picked, swapped)
        keep = (2 * q + lane // 64 == ref_tm) & (lax.rem(lane // 2, 2) == ref_low) & (here == 1)
        left = jnp.where(keep, left, 0.0).astype(BF16)
        columns = columns + lax.dot_general(
            left, block, (((1,), (1,)), ((), ())), preferred_element_type=F32
        )

    inner = lax.rem(s, 8)
    outer = s // 8

    def columns_copy(phase, d):
        if phase == 0:
            to, slot, landing, sem = {"stn": outer * 8 + lax.rem(inner + d, 8)}, inner, cols_a, crs_a
        elif phase == 1:
            to, slot, landing, sem = {"stn": lax.rem(outer + d, 4) * 8 + inner}, outer, cols_b, crs_b
        else:
            to, slot, landing, sem = {"tm": lax.rem(t + d, TM)}, t, cols_c, crs_c
        return pltpu.make_async_remote_copy(
            src_ref=cols_out.at[phase],
            dst_ref=landing.at[slot],
            send_sem=css.at[phase],
            recv_sem=sem.at[0],
            device_id=to,
            device_id_type=MESH,
        )

    for phase, (landing, sem, slot, size) in enumerate(
        ((cols_a, crs_a, inner, 8), (cols_b, crs_b, outer, 4), (cols_c, crs_c, t, TM))
    ):
        low = columns.astype(BF16)
        cols_out[phase] = low
        landing[slot] = low

        @pl.loop(1, size)
        def _(d):
            columns_copy(phase, d).start()

        bytes_of(landing.at[pl.ds(0, size - 1)], sem.at[0])
        columns = landing[0].astype(F32)
        for other in range(1, size):
            columns = columns + landing[other].astype(F32)
    columns = columns * (1.0 / SPECTRA)
    basis_re, basis_im = gram_schmidt(columns[0:K], columns[K:])
    basis[0:K, :] = basis_re
    basis[K:, :] = basis_im

    for phase, size in enumerate((8, 4, TM)):
        bytes_of(cols_a.at[pl.ds(0, size - 1)], css.at[phase])

    @pl.loop(0, NCH)
    def _(j):
        bytes_of(send1.at[j, pl.ds(0, INPUTS - LOCAL)], ss1.at[j])

    @pl.when(t < TM - 1)
    def _():
        @pl.loop(0, NCH)
        def _(j):
            bytes_of(halo_out.at[j], halo_ss.at[j])

    @pl.loop(0, TM)
    def _(other):
        @pl.when(other != t)
        def _():
            bytes_of(send2.at[other], ss2.at[other])
            bytes_of(v.at[other], rs2.at[other])


def channelise(volt, taps, table, ref_chan, basis_in):
    vmem = pl.BlockSpec(memory_space=pltpu.VMEM)
    smem = pl.BlockSpec(memory_space=pltpu.SMEM)
    dma = pltpu.SemaphoreType.DMA
    return pl.pallas_call(
        channelise_kernel,
        out_shape=(
            jax.ShapeDtypeStruct((NCH, INPUTS, WIDE), BF16),
            jax.ShapeDtypeStruct((TM, INPUTS // 2, 128), BF16),
            jax.ShapeDtypeStruct((2 * K, INPUTS), F32),
        ),
        in_specs=[vmem, vmem, pl.BlockSpec(memory_space=pl.ANY), smem, smem],
        out_specs=(vmem, vmem, vmem),
        scratch_shapes=[
            pltpu.VMEM((NCH, 2 * NFFT, 2 * WIDE), BF16),
            pltpu.VMEM((TAPS * Q, 128), F32),
            pltpu.VMEM((FRAMES * LOCAL * Q, 128), F32),
            pltpu.VMEM((FRAMES * LOCAL, 2 * NFFT), BF16),
            pltpu.VMEM((NCH, SPILL * LOCAL, 2 * WIDE), BF16),
            pltpu.VMEM((NCH, SPILL * LOCAL, 2 * WIDE), BF16),
            pltpu.VMEM((NCH, INPUTS, WIDE), BF16),
            pltpu.VMEM((TM, INPUTS // 2, 128), BF16),
            pltpu.VMEM((3, 2 * K, INPUTS), BF16),
            pltpu.VMEM((8, 2 * K, INPUTS), BF16),
            pltpu.VMEM((4, 2 * K, INPUTS), BF16),
            pltpu.VMEM((TM, 2 * K, INPUTS), BF16),
            dma,
            dma((NCH,)),
            dma((NCH,)),
            dma((NCH,)),
            dma((NCH,)),
            dma((TM,)),
            dma((TM,)),
            dma((3,)),
            dma((1,)),
            dma((1,)),
            dma((1,)),
        ],
        compiler_params=pltpu.CompilerParams(
            collective_id=0, has_side_effects=True, vmem_limit_bytes=40 * 1024 * 1024
        ),
        name="channelise",
    )(volt, taps, table, ref_chan, basis_in)


def covariance_kernel(u, v, basis, cov, proj, power):
    lane = lax.broadcasted_iota(jnp.int32, (1, 128), 1)
    lane4 = lax.broadcasted_iota(jnp.int32, (1, 512), 1)
    first = lane < 64
    tops, bottoms = [], []
    for pair in range(TM // 2):
        one, two = v[2 * pair].astype(F32), v[2 * pair + 1].astype(F32)
        tops.append(jnp.where(first, one, pltpu.roll(two, 64, 1)))
        bottoms.append(jnp.where(first, pltpu.roll(one, 64, 1), two))
    x = jnp.concatenate(
        [jnp.concatenate(tops, axis=1), jnp.concatenate(bottoms, axis=1)], axis=0
    )
    real = (lane4 & 1) == 0
    swapped = jnp.where(real, pltpu.roll(x, 511, 1), -pltpu.roll(x, 1, 1))
    x_low, swapped = x.astype(BF16), swapped.astype(BF16)
    for ch in range(2):
        keep = (lane4 & 2) == 2 * ch
        for part, left in enumerate((x_low, swapped)):
            left = jnp.where(keep, left, jnp.zeros_like(left))
            prod = lax.dot_general(
                left, x_low, (((1,), (1,)), ((), ())), preferred_element_type=F32
            )
            cov[ch, :, part * INPUTS : (part + 1) * INPUTS] = (prod * (1.0 / SPECTRA)).astype(BF16)

    b = basis[...]
    b0 = b.astype(BF16)
    rest = b - b0.astype(F32)
    b1 = rest.astype(BF16)
    b2 = (rest - b1.astype(F32)).astype(BF16)
    y = sum(jnp.dot(part, x_low, preferred_element_type=F32) for part in (b2, b1, b0))
    y_re = y[0:K] + pltpu.roll(y[K:], 511, 1)
    y_im = pltpu.roll(y[0:K], 511, 1) - y[K:]
    y = jnp.concatenate([y_re, y_im], axis=0)
    row = lax.broadcasted_iota(jnp.int32, (K, 128), 0)
    col = lax.broadcasted_iota(jnp.int32, (K, 128), 1)
    for ch in range(2):
        left = jnp.where((lane4 & 3) == 2 * ch, y, 0.0)
        gram = lax.dot_general(
            left, y, (((1,), (1,)), ((), ())), precision=HIGHEST, preferred_element_type=F32
        )
        re = gram[0:K, 0:K] + gram[K:, K:]
        im = gram[K:, 0:K] - gram[0:K, K:]
        flat = jnp.concatenate([re] * K + [im] * K, axis=1)
        flat = jnp.where(lax.rem(col // K, K) == row, flat, 0.0)
        proj[ch : ch + 1, :] = jnp.sum(flat, axis=0, keepdims=True) * (1.0 / SPECTRA)

    rows = lax.broadcasted_iota(jnp.int32, (16, 128), 0)
    lanes = lax.broadcasted_iota(jnp.int32, (16, 128), 1)
    spectrum = jnp.where(
        lax.rem(lax.broadcasted_iota(jnp.int32, (128, 16), 0) // 4, 16)
        == lax.broadcasted_iota(jnp.int32, (128, 16), 1),
        1.0,
        0.0,
    )
    total = jnp.zeros((16, 16), F32)
    for q in range(TILES):
        z = jnp.dot(b0, u[q // CH, :, (q % CH) * 128 : (q % CH + 1) * 128], preferred_element_type=F32)
        z_re = z[0:K] + pltpu.roll(z[K:], 127, 1)
        z_im = pltpu.roll(z[0:K], 127, 1) - z[K:]
        squares = jnp.sum(z_re * z_re + z_im * z_im, axis=0, keepdims=True)
        channel = (2 * q + lanes // 64) * 2 + lax.rem(lanes // 2, 2)
        keep = (channel == rows) & ((lanes & 1) == 0)
        total = total + jnp.dot(
            jnp.where(keep, squares, 0.0), spectrum, precision=HIGHEST, preferred_element_type=F32
        )
    power[...] = total


def covariance_of(u, v, basis):
    vmem = pl.BlockSpec(memory_space=pltpu.VMEM)
    return pl.pallas_call(
        covariance_kernel,
        out_shape=(
            jax.ShapeDtypeStruct((2, INPUTS, 2 * INPUTS), BF16),
            jax.ShapeDtypeStruct((2, 2 * K * K), F32),
            jax.ShapeDtypeStruct((16, FRAMES), F32),
        ),
        in_specs=[vmem] * 3,
        out_specs=(vmem,) * 3,
        compiler_params=pltpu.CompilerParams(vmem_limit_bytes=40 * 1024 * 1024),
        name="covariances",
    )(u, v, basis)


def on_device(table, voltages, filter_taps, reference_channel, basis_inputs):
    volt = voltages.reshape(LOCAL, 2, FRAMES * SUB, 128).transpose(0, 2, 1, 3).reshape(-1, 128)
    u, v, basis = channelise(volt, filter_taps, table, reference_channel, basis_inputs)
    return covariance_of(u, v, basis)


def solution(mesh):
    table = transform_table()

    def whole(voltages, filter_taps, reference_channel, basis_inputs):
        return jax.shard_map(
            on_device,
            mesh=mesh,
            in_specs=(P(), P("stn", None, "tm"), P(), P(), P()),
            out_specs=(P(("stn", "tm"), None, None), P(("stn", "tm"), None), P("stn", "tm")),
            check_vma=False,
        )(jnp.asarray(table), voltages, filter_taps, reference_channel, basis_inputs)

    return whole
```

```python
import functools
import math

import jax
import jax.numpy as jnp
import numpy as np
from jax import lax
from jax.experimental import pallas as pl
from jax.experimental.pallas import tpu as pltpu
from jax.sharding import PartitionSpec as P

NFFT = 1024
FCH = 512
TAPS = 16
K = 8
INPUTS = 512
SPECTRA = 128
STN = 32
TM = 8
LOCAL = INPUTS // STN
FRAMES = SPECTRA // TM
SUB = NFFT // 128
Q = 2 * SUB
SPILL = TAPS - 1
VOLT_ROWS = LOCAL * FRAMES * Q
PACE = 1
COLUMNS_AT = 1
PARTS = 4
TILES = 4
CH = 1
NCH = TILES // CH
WIDE = CH * 128
MESH = pl.DeviceIdType.MESH
F32 = jnp.float32
BF16 = jnp.bfloat16
HIGHEST = lax.Precision.HIGHEST


def transform_table():
    phase = np.arange(NFFT)[:, None] * np.arange(FCH)[None, :] % NFFT
    angle = phase.astype(np.float32) * np.float32(2.0 * math.pi / NFFT)
    factor = np.float32(1.0 / math.sqrt(NFFT))
    cosine, sine = np.cos(angle) * factor, np.sin(angle) * factor
    table_re = np.stack([cosine, -sine], axis=2)
    table_im = np.stack([sine, cosine], axis=2)
    both = np.stack([table_re.reshape(SUB, 128, FCH, 2), table_im.reshape(SUB, 128, FCH, 2)], axis=1)
    both = both.reshape(2 * NFFT, 2, 16, TILES, 2, 2, 2)
    both = both.transpose(3, 0, 1, 4, 2, 5, 6)
    both = both.reshape(NCH, CH, 2 * NFFT, 256).transpose(0, 2, 1, 3)
    return both.reshape(NCH, 2 * NFFT, 2 * WIDE).astype(jnp.bfloat16)


def butterfly(blocks, lane):
    blocks = list(blocks)
    for bit in range(4):
        step, shift = 1 << bit, 4 << bit
        low = (lane & shift) == 0
        for a in range(16):
            if a & step:
                continue
            first, second = blocks[a], blocks[a | step]
            blocks[a] = jnp.where(low, first, pltpu.roll(second, shift, 1))
            blocks[a | step] = jnp.where(low, pltpu.roll(first, 128 - shift, 1), second)
    return blocks


def gram_schmidt(vec_re, vec_im):
    row = lax.broadcasted_iota(jnp.int32, (K, 1), 0)
    for k in range(K):
        w_re, w_im = vec_re[k : k + 1], vec_im[k : k + 1]
        in_re = jnp.sum(w_re * vec_re + w_im * vec_im, axis=1, keepdims=True)
        in_im = jnp.sum(w_re * vec_im - w_im * vec_re, axis=1, keepdims=True)
        inverse = lax.rsqrt(in_re[k : k + 1] + 1e-06)
        q_re, q_im = w_re * inverse, w_im * inverse
        c_re = jnp.where(row > k, in_re * inverse, 0.0)
        c_im = jnp.where(row > k, in_im * inverse, 0.0)
        new_re = vec_re - (q_re * c_re - q_im * c_im)
        new_im = vec_im - (q_re * c_im + q_im * c_re)
        vec_re = jnp.where(row == k, q_re, new_re)
        vec_im = jnp.where(row == k, q_im, new_im)
    return vec_re, vec_im


def channelise_kernel(
    volt_hbm, taps_hbm, table_hbm, ref_hbm, basis_hbm,
    u, v, basis,
    volt, taps, ref_chan, basis_in, table, tap_rows, frames_f, lhs, halo_out, halo_in, send1, send2, ref_halo, ref_out, ref_in, cols_out, cols_in,
    volt_sem, small_sem, table_sem, halo_ss, halo_rs, ss1, rs1, ss2, rs2, ref_sem, cols_sem,
):
    s = lax.axis_index("stn")
    t = lax.axis_index("tm")
    load_taps = pltpu.make_async_copy(taps_hbm, taps, small_sem.at[0])
    load_taps.start()
    load_ref = pltpu.make_async_copy(ref_hbm, ref_chan, small_sem.at[1])
    load_ref.start()
    load_basis = pltpu.make_async_copy(basis_hbm, basis_in, small_sem.at[2])
    load_basis.start()

    def load_volt(part):
        rows = pl.ds(pl.multiple_of(part * (VOLT_ROWS // PARTS), 8), VOLT_ROWS // PARTS)
        return pltpu.make_async_copy(volt_hbm.at[rows], volt.at[rows], volt_sem.at[part])

    for part in range(PARTS):
        load_volt(part).start()
    load_table = pltpu.make_async_copy(table_hbm, table, table_sem)
    load_table.start()

    barrier = pltpu.get_barrier_semaphore()

    @pl.loop(1, STN)
    def _(d):
        pl.semaphore_signal(barrier, 1, device_id={"stn": lax.rem(s + d, STN)}, device_id_type=MESH)

    @pl.loop(1, TM)
    def _(d):
        pl.semaphore_signal(barrier, 1, device_id={"tm": lax.rem(t + d, TM)}, device_id_type=MESH)

    load_taps.wait()
    for sub in range(SUB):
        part = taps[:, sub * 128 : (sub + 1) * 128] * (1.0 / 64.0)
        for p in range(2):
            tap_rows[pl.ds(sub * 2 + p, TAPS, stride=Q), :] = part

    def filter_frames(spill):
        @pl.loop(0, LOCAL * 2)
        def _(step):
            if spill:
                @pl.when(lax.rem(step, LOCAL * 2 // PARTS) == 0)
                def _():
                    load_volt(step // (LOCAL * 2 // PARTS)).wait()

            i, half = step // 2, lax.rem(step, 2)
            base = pl.multiple_of(i * (FRAMES * Q) + half * 8, 8)
            x = [volt[pl.ds(base + f * Q, 8), :].astype(F32) for f in range(FRAMES)]
            tap = [tap_rows[pl.ds(pl.multiple_of(k * Q + half * 8, 8), 8), :] for k in range(TAPS)]
            for f in range(SPILL if spill else FRAMES):
                acc = None
                for j in range(f + 1, FRAMES) if spill else range(f + 1):
                    k = j - f - 1 if spill else SPILL - f + j
                    term = tap[k] * x[j]
                    acc = term if acc is None else acc + term
                row = pl.multiple_of((f * LOCAL + i) * Q + half * 8, 8)
                frames_f[pl.ds(row, 8), :] = acc

        rows = (SPILL if spill else FRAMES) * LOCAL
        for q in range(Q):
            lhs[0:rows, q * 128 : (q + 1) * 128] = frames_f[pl.ds(q, rows, stride=Q), :].astype(BF16)

    def chunk_of(block, step):
        return lax.rem(block // (2 * CH) + 1 + step, NCH)

    def halo_copy(j):
        return pltpu.make_async_remote_copy(
            src_ref=halo_out.at[j],
            dst_ref=halo_in.at[j],
            send_sem=halo_ss.at[j],
            recv_sem=halo_rs.at[j],
            device_id={"tm": lax.rem(t + 1, TM)},
            device_id_type=MESH,
        )

    def stage1_copy(j, to):
        return pltpu.make_async_remote_copy(
            src_ref=send1.at[j, pl.ds(pl.multiple_of(to * LOCAL, LOCAL), LOCAL)],
            dst_ref=u.at[j, pl.ds(pl.multiple_of(s * LOCAL, LOCAL), LOCAL)],
            send_sem=ss1.at[j],
            recv_sem=rs1.at[j],
            device_id={"stn": to},
            device_id_type=MESH,
        )

    def stage2_copy(to):
        return pltpu.make_async_remote_copy(
            src_ref=send2.at[to],
            dst_ref=v.at[t],
            send_sem=ss2.at[to],
            recv_sem=rs2.at[t],
            device_id={"tm": to},
            device_id_type=MESH,
        )

    def bytes_of(ref, sem):
        pltpu.make_async_copy(ref, ref, sem).wait()

    lane = lax.broadcasted_iota(jnp.int32, (1, 128), 1)

    def ref_tile(rows, ref_table):
        part = jnp.dot(lhs[0 : rows * LOCAL, :], ref_table, preferred_element_type=F32)
        total = jnp.zeros((LOCAL, 128), F32)
        for f in range(rows):
            total = total + jnp.where(
                lax.rem(lane // 2, FRAMES) == f, part[f * LOCAL : (f + 1) * LOCAL], 0.0
            )
        return total

    def ref_halo_copy():
        return pltpu.make_async_remote_copy(
            src_ref=ref_halo.at[0],
            dst_ref=ref_halo.at[1],
            send_sem=ref_sem.at[0],
            recv_sem=ref_sem.at[1],
            device_id={"tm": lax.rem(t + 1, TM)},
            device_id_type=MESH,
        )

    def ref_copy(to):
        return pltpu.make_async_remote_copy(
            src_ref=ref_out,
            dst_ref=ref_in.at[pl.ds(pl.multiple_of(s * LOCAL, LOCAL), LOCAL)],
            send_sem=ref_sem.at[2],
            recv_sem=ref_sem.at[3],
            device_id={"stn": to},
            device_id_type=MESH,
        )

    def columns_copy(to):
        return pltpu.make_async_remote_copy(
            src_ref=cols_out,
            dst_ref=cols_in.at[t],
            send_sem=cols_sem.at[0],
            recv_sem=cols_sem.at[1],
            device_id={"tm": to},
            device_id_type=MESH,
        )

    def next_halo(step):
        if step >= NCH:
            return

        @pl.when(t < TM - 1)
        def _():
            if step >= PACE:
                before = chunk_of(lax.rem(t + 1, TM), step - PACE)
                bytes_of(halo_out.at[before], halo_ss.at[before])
            halo_copy(chunk_of(lax.rem(t + 1, TM), step)).start()

    filter_frames(True)
    load_table.wait()
    load_ref.wait()
    load_basis.wait()
    ref = ref_chan[0]
    ref_stn, ref_tm, ref_low = ref // 16, lax.rem(ref // 2, TM), lax.rem(ref, 2)
    ref_at = (lax.rem(ref_tm // 2, CH) * 2 + ref_stn // 16) * 128
    ref_at = ref_at + lax.rem(ref_tm, 2) * 64 + lax.rem(ref_stn, 16) * 4 + ref_low * 2
    chosen = lax.broadcasted_iota(jnp.int32, (2 * WIDE, 128), 0) == ref_at + (lane & 1)
    ref_table = jnp.dot(
        table[ref_tm // (2 * CH)],
        jnp.where(chosen, 1.0, 0.0).astype(BF16),
        preferred_element_type=F32,
    ).astype(BF16)
    ref_halo[0] = ref_tile(SPILL, ref_table).astype(BF16)
    for step in range(NCH):
        j = chunk_of(lax.rem(t + 1, TM), step)
        part = jnp.dot(lhs[0 : SPILL * LOCAL, :], table[j], preferred_element_type=F32)
        halo_out[j] = part.astype(BF16)

    pl.semaphore_wait(barrier, STN - 1 + TM - 1)

    @pl.when(t < TM - 1)
    def _():
        ref_halo_copy().start()

    for step in range(PACE):
        next_halo(step)

    filter_frames(False)

    @pl.when(t == 0)
    def _():
        halo_in[...] = jnp.zeros_like(halo_in)
        ref_halo[1] = jnp.zeros((LOCAL, 128), BF16)

    own_ref = ref_tile(FRAMES, ref_table)

    @pl.when(t > 0)
    def _():
        bytes_of(ref_halo.at[1], ref_sem.at[1])

    ref_out[...] = (own_ref + ref_halo[1].astype(F32)).astype(BF16)
    ref_in[pl.ds(pl.multiple_of(s * LOCAL, LOCAL), LOCAL), :] = ref_out[...]

    @pl.loop(1, STN)
    def _(d):
        ref_copy(lax.rem(s + d, STN)).start()

    next_halo(PACE)

    def stage1(step):
        j = chunk_of(t, step)
        own = jnp.dot(lhs[...], table[j], preferred_element_type=F32)

        @pl.when(t > 0)
        def _():
            bytes_of(halo_in.at[j], halo_rs.at[j])

        head = own[0 : SPILL * LOCAL] + halo_in[j].astype(F32)
        own = jnp.concatenate([head, own[SPILL * LOCAL :]], axis=0)
        own = own.astype(BF16).astype(F32)
        for c in range(CH):
            for hi in range(2):
                at = (c * 2 + hi) * 128
                blocks = [own[f * LOCAL : (f + 1) * LOCAL, at : at + 128] for f in range(FRAMES)]
                for g, block in enumerate(butterfly(blocks, lane)):
                    row = (hi * 16 + g) * LOCAL
                    send1[j, row : row + LOCAL, c * 128 : (c + 1) * 128] = block.astype(BF16)
        mine = pl.ds(pl.multiple_of(s * LOCAL, LOCAL), LOCAL)
        u[j, mine, :] = send1[j, mine, :]

        @pl.loop(1, STN)
        def _(d):
            stage1_copy(j, lax.rem(s + d, STN)).start()

    def stage2(step):
        j = chunk_of(t, step)
        bytes_of(u.at[j, pl.ds(0, INPUTS - LOCAL)], rs1.at[j])
        for c in range(CH):
            block = u[j, :, c * 128 : (c + 1) * 128].astype(F32)
            low, high = block[0 : INPUTS // 2], block[INPUTS // 2 :]
            first = lane < 64
            pair = (
                jnp.where(first, low, pltpu.roll(high, 64, 1)),
                jnp.where(first, pltpu.roll(low, 64, 1), high),
            )
            for b in range(2):
                to = (j * CH + c) * 2 + b
                send2[to] = pair[b].astype(BF16)

                @pl.when(to != t)
                def _():
                    stage2_copy(to).start()

    def send_columns():
        bytes_of(ref_in.at[pl.ds(0, INPUTS - LOCAL)], ref_sem.at[3])
        row16 = lax.broadcasted_iota(jnp.int32, (2 * K, 1), 0)
        wanted = jnp.zeros((2 * K, 1), jnp.int32)
        for k in range(K):
            wanted = jnp.where(lax.rem(row16, K) == k, basis_in[k], wanted)
        column = lax.broadcasted_iota(jnp.int32, (2 * K, INPUTS), 1)
        onehot = jnp.where(column == wanted, 1.0, 0.0).astype(BF16)
        block = ref_in[...]
        picked = jnp.dot(onehot, block, preferred_element_type=F32)
        swapped = jnp.where((lane & 1) == 0, -pltpu.roll(picked, 127, 1), pltpu.roll(picked, 1, 1))
        left = jnp.where(row16 < K, picked, swapped)
        left = jnp.where(lane < 2 * FRAMES, left, 0.0).astype(BF16)
        columns = lax.dot_general(
            left, block, (((1,), (1,)), ((), ())), preferred_element_type=F32
        ).astype(BF16)
        cols_out[...] = columns
        cols_in[t] = columns

        @pl.loop(1, TM)
        def _(d):
            columns_copy(lax.rem(t + d, TM)).start()

    def find_basis():
        bytes_of(cols_in.at[pl.ds(0, TM - 1)], cols_sem.at[1])
        columns = cols_in[0].astype(F32)
        for other in range(1, TM):
            columns = columns + cols_in[other].astype(F32)
        columns = columns * (1.0 / SPECTRA)
        basis_re, basis_im = gram_schmidt(columns[0:K], columns[K:])
        basis[0:K, :] = basis_re
        basis[K:, :] = basis_im

    for step in range(NCH):
        stage1(step)
        next_halo(PACE + 1 + step)
        if step > 0:
            stage2(step - 1)
        if step == COLUMNS_AT:
            send_columns()
    find_basis()
    stage2(NCH - 1)
    v[t] = send2[t]

    bytes_of(cols_in.at[pl.ds(0, TM - 1)], cols_sem.at[0])
    bytes_of(ref_in.at[pl.ds(0, INPUTS - LOCAL)], ref_sem.at[2])

    @pl.loop(0, NCH)
    def _(j):
        bytes_of(send1.at[j, pl.ds(0, INPUTS - LOCAL)], ss1.at[j])

    @pl.when(t < TM - 1)
    def _():
        bytes_of(ref_halo.at[0], ref_sem.at[0])
        for step in range(NCH - PACE, NCH):
            j = chunk_of(lax.rem(t + 1, TM), step)
            bytes_of(halo_out.at[j], halo_ss.at[j])

    @pl.loop(0, TM)
    def _(other):
        @pl.when(other != t)
        def _():
            bytes_of(send2.at[other], ss2.at[other])
            bytes_of(v.at[other], rs2.at[other])


def channelise(volt, taps, table, ref_chan, basis_in):
    vmem = pl.BlockSpec(memory_space=pltpu.VMEM)
    hbm = pl.BlockSpec(memory_space=pltpu.HBM)
    dma = pltpu.SemaphoreType.DMA
    return pl.pallas_call(
        channelise_kernel,
        out_shape=(
            jax.ShapeDtypeStruct((NCH, INPUTS, WIDE), BF16),
            jax.ShapeDtypeStruct((TM, INPUTS // 2, 128), BF16),
            jax.ShapeDtypeStruct((2 * K, INPUTS), F32),
        ),
        in_specs=[hbm] * 5,
        out_specs=(vmem, vmem, vmem),
        scratch_shapes=[
            pltpu.VMEM((VOLT_ROWS, 128), jnp.int32),
            pltpu.VMEM((TAPS, NFFT), F32),
            pltpu.SMEM((1,), jnp.int32),
            pltpu.SMEM((K,), jnp.int32),
            pltpu.VMEM((NCH, 2 * NFFT, 2 * WIDE), BF16),
            pltpu.VMEM((TAPS * Q, 128), F32),
            pltpu.VMEM((FRAMES * LOCAL * Q, 128), F32),
            pltpu.VMEM((FRAMES * LOCAL, 2 * NFFT), BF16),
            pltpu.VMEM((NCH, SPILL * LOCAL, 2 * WIDE), BF16),
            pltpu.VMEM((NCH, SPILL * LOCAL, 2 * WIDE), BF16),
            pltpu.VMEM((NCH, INPUTS, WIDE), BF16),
            pltpu.VMEM((TM, INPUTS // 2, 128), BF16),
            pltpu.VMEM((2, LOCAL, 128), BF16),
            pltpu.VMEM((LOCAL, 128), BF16),
            pltpu.VMEM((INPUTS, 128), BF16),
            pltpu.VMEM((2 * K, INPUTS), BF16),
            pltpu.VMEM((TM, 2 * K, INPUTS), BF16),
            dma((PARTS,)),
            dma((3,)),
            dma,
            dma((NCH,)),
            dma((NCH,)),
            dma((NCH,)),
            dma((NCH,)),
            dma((TM,)),
            dma((TM,)),
            dma((4,)),
            dma((2,)),
        ],
        compiler_params=pltpu.CompilerParams(
            collective_id=0, has_side_effects=True, vmem_limit_bytes=40 * 1024 * 1024
        ),
        name="channelise",
    )(volt, taps, table, ref_chan, basis_in)


def covariance_kernel(u, v, basis, cov, proj, power):
    lane = lax.broadcasted_iota(jnp.int32, (1, 128), 1)
    lane4 = lax.broadcasted_iota(jnp.int32, (1, 512), 1)
    first = lane < 64
    tops, bottoms = [], []
    for pair in range(TM // 2):
        one, two = v[2 * pair].astype(F32), v[2 * pair + 1].astype(F32)
        tops.append(jnp.where(first, one, pltpu.roll(two, 64, 1)))
        bottoms.append(jnp.where(first, pltpu.roll(one, 64, 1), two))
    x = jnp.concatenate(
        [jnp.concatenate(tops, axis=1), jnp.concatenate(bottoms, axis=1)], axis=0
    )
    real = (lane4 & 1) == 0
    swapped = jnp.where(real, pltpu.roll(x, 511, 1), -pltpu.roll(x, 1, 1))
    x_low, swapped = x.astype(BF16), swapped.astype(BF16)
    for ch in range(2):
        keep = (lane4 & 2) == 2 * ch
        for part, left in enumerate((x_low, swapped)):
            left = jnp.where(keep, left, jnp.zeros_like(left))
            prod = lax.dot_general(
                left, x_low, (((1,), (1,)), ((), ())), preferred_element_type=F32
            )
            cov[ch, :, part * INPUTS : (part + 1) * INPUTS] = (prod * (1.0 / SPECTRA)).astype(BF16)

    b = basis[...]
    b0 = b.astype(BF16)
    rest = b - b0.astype(F32)
    b1 = rest.astype(BF16)
    b2 = (rest - b1.astype(F32)).astype(BF16)
    y = sum(jnp.dot(part, x_low, preferred_element_type=F32) for part in (b2, b1, b0))
    y_re = y[0:K] + pltpu.roll(y[K:], 511, 1)
    y_im = pltpu.roll(y[0:K], 511, 1) - y[K:]
    y = jnp.concatenate([y_re, y_im], axis=0)
    row = lax.broadcasted_iota(jnp.int32, (K, 128), 0)
    col = lax.broadcasted_iota(jnp.int32, (K, 128), 1)
    for ch in range(2):
        left = jnp.where((lane4 & 3) == 2 * ch, y, 0.0)
        gram = lax.dot_general(
            left, y, (((1,), (1,)), ((), ())), precision=HIGHEST, preferred_element_type=F32
        )
        re = gram[0:K, 0:K] + gram[K:, K:]
        im = gram[K:, 0:K] - gram[0:K, K:]
        flat = jnp.concatenate([re] * K + [im] * K, axis=1)
        flat = jnp.where(lax.rem(col // K, K) == row, flat, 0.0)
        proj[ch : ch + 1, :] = jnp.sum(flat, axis=0, keepdims=True) * (1.0 / SPECTRA)

    rows = lax.broadcasted_iota(jnp.int32, (16, 128), 0)
    lanes = lax.broadcasted_iota(jnp.int32, (16, 128), 1)
    spectrum = jnp.where(
        lax.rem(lax.broadcasted_iota(jnp.int32, (128, 16), 0) // 4, 16)
        == lax.broadcasted_iota(jnp.int32, (128, 16), 1),
        1.0,
        0.0,
    )
    total = jnp.zeros((16, 16), F32)
    for q in range(TILES):
        z = jnp.dot(b0, u[q // CH, :, (q % CH) * 128 : (q % CH + 1) * 128], preferred_element_type=F32)
        z_re = z[0:K] + pltpu.roll(z[K:], 127, 1)
        z_im = pltpu.roll(z[0:K], 127, 1) - z[K:]
        squares = jnp.sum(z_re * z_re + z_im * z_im, axis=0, keepdims=True)
        channel = (2 * q + lanes // 64) * 2 + lax.rem(lanes // 2, 2)
        keep = (channel == rows) & ((lanes & 1) == 0)
        total = total + jnp.dot(
            jnp.where(keep, squares, 0.0), spectrum, precision=HIGHEST, preferred_element_type=F32
        )
    power[...] = total


def covariance_of(u, v, basis):
    vmem = pl.BlockSpec(memory_space=pltpu.VMEM)
    return pl.pallas_call(
        covariance_kernel,
        out_shape=(
            jax.ShapeDtypeStruct((2, INPUTS, 2 * INPUTS), BF16),
            jax.ShapeDtypeStruct((2, 2 * K * K), F32),
            jax.ShapeDtypeStruct((16, FRAMES), F32),
        ),
        in_specs=[vmem] * 3,
        out_specs=(vmem,) * 3,
        compiler_params=pltpu.CompilerParams(vmem_limit_bytes=40 * 1024 * 1024),
        name="covariances",
    )(u, v, basis)


def on_device(table, voltages, filter_taps, reference_channel, basis_inputs):
    volt = voltages.reshape(LOCAL, 2, FRAMES * SUB, 128).transpose(0, 2, 1, 3).reshape(-1, 128)
    u, v, basis = channelise(volt, filter_taps, table, reference_channel, basis_inputs)
    return covariance_of(u, v, basis)


def solution(mesh):
    table = transform_table()

    def whole(voltages, filter_taps, reference_channel, basis_inputs):
        return jax.shard_map(
            on_device,
            mesh=mesh,
            in_specs=(P(), P("stn", None, "tm"), P(), P(), P()),
            out_specs=(P(("stn", "tm"), None, None), P(("stn", "tm"), None), P("stn", "tm")),
            check_vma=False,
        )(jnp.asarray(table), voltages, filter_taps, reference_channel, basis_inputs)

    return whole
```

```python
import functools
import math

import jax
import jax.numpy as jnp
import numpy as np
from jax import lax
from jax.experimental import pallas as pl
from jax.experimental.pallas import tpu as pltpu
from jax.sharding import PartitionSpec as P

NFFT = 1024
FCH = 512
TAPS = 16
K = 8
INPUTS = 512
SPECTRA = 128
STN = 32
TM = 8
LOCAL = INPUTS // STN
FRAMES = SPECTRA // TM
SUB = NFFT // 128
Q = 2 * SUB
SPILL = TAPS - 1
VOLT_ROWS = LOCAL * FRAMES * Q
COLUMNS_AT = 1
PARTS = 4
PIECES = 4
TILES = TM // 2
OWN_ROWS, SPILL_ROWS = FRAMES * LOCAL, SPILL * LOCAL
LIMIT = 60
MESH = pl.DeviceIdType.MESH
F32 = jnp.float32
BF16 = jnp.bfloat16
HIGHEST = lax.Precision.HIGHEST


def transform_table():
    phase = np.arange(NFFT)[:, None] * np.arange(FCH)[None, :] % NFFT
    angle = phase.astype(np.float32) * np.float32(2.0 * math.pi / NFFT)
    factor = np.float32(1.0 / math.sqrt(NFFT))
    cosine, sine = np.cos(angle) * factor, np.sin(angle) * factor
    table_re = np.stack([cosine, -sine], axis=2)
    table_im = np.stack([sine, cosine], axis=2)
    both = np.stack([table_re.reshape(SUB, 128, FCH, 2), table_im.reshape(SUB, 128, FCH, 2)], axis=1)
    both = both.reshape(2 * NFFT, STN, PIECES, 2, 2, 2)
    both = both.transpose(2, 0, 3, 1, 4, 5)
    return both.reshape(PIECES, 2 * NFFT, 256).astype(jnp.bfloat16)


def butterfly(blocks, lane):
    blocks = list(blocks)
    for bit in range(5):
        step, shift = 1 << bit, 4 << bit
        low = (lane & shift) == 0
        for a in range(32):
            if a & step:
                continue
            first, second = blocks[a], blocks[a | step]
            blocks[a] = jnp.where(low, first, pltpu.roll(second, shift, 1))
            blocks[a | step] = jnp.where(low, pltpu.roll(first, 128 - shift, 1), second)
    return blocks


def gram_schmidt(vec_re, vec_im):
    row = lax.broadcasted_iota(jnp.int32, (K, 1), 0)
    for k in range(K):
        w_re, w_im = vec_re[k : k + 1], vec_im[k : k + 1]
        in_re = jnp.sum(w_re * vec_re + w_im * vec_im, axis=1, keepdims=True)
        in_im = jnp.sum(w_re * vec_im - w_im * vec_re, axis=1, keepdims=True)
        inverse = lax.rsqrt(in_re[k : k + 1] + 1e-06)
        q_re, q_im = w_re * inverse, w_im * inverse
        c_re = jnp.where(row > k, in_re * inverse, 0.0)
        c_im = jnp.where(row > k, in_im * inverse, 0.0)
        new_re = vec_re - (q_re * c_re - q_im * c_im)
        new_im = vec_im - (q_re * c_im + q_im * c_re)
        vec_re = jnp.where(row == k, q_re, new_re)
        vec_im = jnp.where(row == k, q_im, new_im)
    return vec_re, vec_im


def covariances(v, basis, cov, proj):
    lane4 = lax.broadcasted_iota(jnp.int32, (1, 512), 1)
    x = jnp.concatenate([v[m].astype(F32) for m in range(TILES)], axis=1)
    real = (lane4 & 1) == 0
    swapped = jnp.where(real, pltpu.roll(x, 511, 1), -pltpu.roll(x, 1, 1))
    x_low, swapped = x.astype(BF16), swapped.astype(BF16)
    for ch in range(2):
        keep = (lane4 & 2) == 2 * ch
        for part, left in enumerate((x_low, swapped)):
            left = jnp.where(keep, left, jnp.zeros_like(left))
            prod = lax.dot_general(
                left, x_low, (((1,), (1,)), ((), ())), preferred_element_type=F32
            )
            cov[ch, :, part * INPUTS : (part + 1) * INPUTS] = (prod * (1.0 / SPECTRA)).astype(BF16)

    b = basis[...]
    b0 = b.astype(BF16)
    rest = b - b0.astype(F32)
    b1 = rest.astype(BF16)
    b2 = (rest - b1.astype(F32)).astype(BF16)
    y = sum(jnp.dot(part, x_low, preferred_element_type=F32) for part in (b2, b1, b0))
    y_re = y[0:K] + pltpu.roll(y[K:], 511, 1)
    y_im = pltpu.roll(y[0:K], 511, 1) - y[K:]
    y = jnp.concatenate([y_re, y_im], axis=0)
    row = lax.broadcasted_iota(jnp.int32, (K, 128), 0)
    col = lax.broadcasted_iota(jnp.int32, (K, 128), 1)
    for ch in range(2):
        left = jnp.where((lane4 & 3) == 2 * ch, y, 0.0)
        gram = lax.dot_general(
            left, y, (((1,), (1,)), ((), ())), precision=HIGHEST, preferred_element_type=F32
        )
        re = gram[0:K, 0:K] + gram[K:, K:]
        im = gram[K:, 0:K] - gram[0:K, K:]
        flat = jnp.concatenate([re] * K + [im] * K, axis=1)
        flat = jnp.where(lax.rem(col // K, K) == row, flat, 0.0)
        proj[ch : ch + 1, :] = jnp.sum(flat, axis=0, keepdims=True) * (1.0 / SPECTRA)


def channelise_kernel(
    volt_hbm, taps_hbm, table_hbm, ref_hbm, basis_hbm,
    cov, proj, power,
    volt, taps, ref_chan, basis_in, table, tap_rows, frames_f, lhs, spill_out, spill_in, own_out, own_in,
    v, basis, send1, ref_halo, ref_out, ref_in, cols_out, cols_in, pow_out, pow_in,
    volt_sem, small_sem, table_sem, spill_ss, spill_rs, own_ss, own_rs, ss1, rs1, ref_sem, cols_sem, pow_ss, pow_rs,
):
    s = lax.axis_index("stn")
    t = lax.axis_index("tm")
    load_taps = pltpu.make_async_copy(taps_hbm, taps, small_sem.at[0])
    load_taps.start()
    load_ref = pltpu.make_async_copy(ref_hbm, ref_chan, small_sem.at[1])
    load_ref.start()
    load_basis = pltpu.make_async_copy(basis_hbm, basis_in, small_sem.at[2])
    load_basis.start()

    def load_volt(part):
        rows = pl.ds(pl.multiple_of(part * (VOLT_ROWS // PARTS), 8), VOLT_ROWS // PARTS)
        return pltpu.make_async_copy(volt_hbm.at[rows], volt.at[rows], volt_sem.at[part])

    for part in range(PARTS):
        load_volt(part).start()
    load_table = pltpu.make_async_copy(table_hbm, table, table_sem)
    load_table.start()

    barrier = pltpu.get_barrier_semaphore()

    @pl.loop(1, STN)
    def _(d):
        pl.semaphore_signal(barrier, 1, device_id={"stn": lax.rem(s + d, STN)}, device_id_type=MESH)

    @pl.loop(1, TM)
    def _(d):
        pl.semaphore_signal(barrier, 1, device_id={"tm": lax.rem(t + d, TM)}, device_id_type=MESH)

    load_taps.wait()
    for sub in range(SUB):
        part = taps[:, sub * 128 : (sub + 1) * 128] * (1.0 / 64.0)
        for p in range(2):
            tap_rows[pl.ds(sub * 2 + p, TAPS, stride=Q), :] = part

    def filter_frames(spill):
        @pl.loop(0, LOCAL * 2)
        def _(step):
            if spill:
                @pl.when(lax.rem(step, LOCAL * 2 // PARTS) == 0)
                def _():
                    load_volt(step // (LOCAL * 2 // PARTS)).wait()

            i, half = step // 2, lax.rem(step, 2)
            base = pl.multiple_of(i * (FRAMES * Q) + half * 8, 8)
            x = [volt[pl.ds(base + f * Q, 8), :].astype(F32) for f in range(FRAMES)]
            tap = [tap_rows[pl.ds(pl.multiple_of(k * Q + half * 8, 8), 8), :] for k in range(TAPS)]
            for f in range(SPILL if spill else FRAMES):
                acc = None
                for j in range(f + 1, FRAMES) if spill else range(f + 1):
                    k = j - f - 1 if spill else SPILL - f + j
                    term = tap[k] * x[j]
                    acc = term if acc is None else acc + term
                row = pl.multiple_of((f * LOCAL + i) * Q + half * 8, 8)
                frames_f[pl.ds(row, 8), :] = acc

        rows = (SPILL if spill else FRAMES) * LOCAL
        for q in range(Q):
            lhs[0:rows, q * 128 : (q + 1) * 128] = frames_f[pl.ds(q, rows, stride=Q), :].astype(BF16)

    def spill_copy(to):
        return pltpu.make_async_remote_copy(
            src_ref=spill_out.at[to],
            dst_ref=spill_in.at[lax.rem(t + 1, TM)],
            send_sem=spill_ss,
            recv_sem=spill_rs.at[lax.rem(t + 1, TM)],
            device_id={"tm": to},
            device_id_type=MESH,
        )

    def own_copy(to):
        return pltpu.make_async_remote_copy(
            src_ref=own_out.at[to],
            dst_ref=own_in.at[t],
            send_sem=own_ss,
            recv_sem=own_rs.at[t],
            device_id={"tm": to},
            device_id_type=MESH,
        )

    def turn_copy(m, to):
        return pltpu.make_async_remote_copy(
            src_ref=send1.at[m, pl.ds(pl.multiple_of(to * LOCAL, LOCAL), LOCAL)],
            dst_ref=v.at[m, pl.ds(pl.multiple_of(s * LOCAL, LOCAL), LOCAL)],
            send_sem=ss1.at[m],
            recv_sem=rs1.at[m],
            device_id={"stn": to},
            device_id_type=MESH,
        )

    def power_copy(to):
        return pltpu.make_async_remote_copy(
            src_ref=pow_out.at[to],
            dst_ref=pow_in.at[t],
            send_sem=pow_ss,
            recv_sem=pow_rs,
            device_id={"tm": to},
            device_id_type=MESH,
        )

    def bytes_of(ref, sem):
        pltpu.make_async_copy(ref, ref, sem).wait()

    lane = lax.broadcasted_iota(jnp.int32, (1, 128), 1)

    def ref_tile(rows, ref_table):
        part = jnp.dot(lhs[0 : rows * LOCAL, :], ref_table, preferred_element_type=F32)
        total = jnp.zeros((LOCAL, 128), F32)
        for f in range(rows):
            total = total + jnp.where(
                lax.rem(lane // 2, FRAMES) == f, part[f * LOCAL : (f + 1) * LOCAL], 0.0
            )
        return total

    def ref_halo_copy():
        return pltpu.make_async_remote_copy(
            src_ref=ref_halo.at[0],
            dst_ref=ref_halo.at[1],
            send_sem=ref_sem.at[0],
            recv_sem=ref_sem.at[1],
            device_id={"tm": lax.rem(t + 1, TM)},
            device_id_type=MESH,
        )

    def ref_copy(to):
        return pltpu.make_async_remote_copy(
            src_ref=ref_out,
            dst_ref=ref_in.at[pl.ds(pl.multiple_of(s * LOCAL, LOCAL), LOCAL)],
            send_sem=ref_sem.at[2],
            recv_sem=ref_sem.at[3],
            device_id={"stn": to},
            device_id_type=MESH,
        )

    def columns_copy(to):
        return pltpu.make_async_remote_copy(
            src_ref=cols_out,
            dst_ref=cols_in.at[t],
            send_sem=cols_sem.at[0],
            recv_sem=cols_sem.at[1],
            device_id={"tm": to},
            device_id_type=MESH,
        )

    filter_frames(True)
    load_table.wait()
    load_ref.wait()
    load_basis.wait()
    ref = ref_chan[0]
    ref_stn, ref_tm, ref_low = ref // 16, lax.rem(ref // 2, TM), lax.rem(ref, 2)
    ref_at = lax.rem(ref_tm, 2) * 128 + ref_stn * 4 + ref_low * 2
    chosen = lax.broadcasted_iota(jnp.int32, (256, 128), 0) == ref_at + (lane & 1)
    ref_table = jnp.dot(
        table[ref_tm // 2],
        jnp.where(chosen, 1.0, 0.0).astype(BF16),
        preferred_element_type=F32,
    ).astype(BF16)
    ref_halo[0] = ref_tile(SPILL, ref_table).astype(BF16)
    for piece in range(PIECES):
        part = jnp.dot(lhs[0:SPILL_ROWS, :], table[piece], preferred_element_type=F32).astype(BF16)
        spill_out[2 * piece] = part[:, 0:128]
        spill_out[2 * piece + 1] = part[:, 128:]

    @pl.when(t < TM - 1)
    def _():
        spill_in[t + 1] = spill_out[t]

    spill_in[0] = jnp.zeros((SPILL_ROWS, 128), BF16)

    pl.semaphore_wait(barrier, STN - 1 + TM - 1)

    @pl.when(t < TM - 1)
    def _():
        ref_halo_copy().start()

        @pl.loop(1, TM)
        def _(d):
            spill_copy(lax.rem(t + d, TM)).start()

    filter_frames(False)

    for step in range(PIECES):
        piece = lax.rem(t // 2 + 1 + step, PIECES)
        part = jnp.dot(lhs[...], table[piece], preferred_element_type=F32).astype(BF16)
        for b in range(2):
            to = 2 * piece + b
            own_out[to] = part[:, b * 128 : (b + 1) * 128]

            @pl.when(to != t)
            def _():
                own_copy(to).start()

    own_in[t] = own_out[t]

    @pl.when(t == 0)
    def _():
        ref_halo[1] = jnp.zeros((LOCAL, 128), BF16)

    own_ref = ref_tile(FRAMES, ref_table)

    @pl.when(t > 0)
    def _():
        bytes_of(ref_halo.at[1], ref_sem.at[1])

    ref_out[...] = (own_ref + ref_halo[1].astype(F32)).astype(BF16)
    ref_in[pl.ds(pl.multiple_of(s * LOCAL, LOCAL), LOCAL), :] = ref_out[...]

    @pl.loop(1, STN)
    def _(d):
        ref_copy(lax.rem(s + d, STN)).start()

    def turn(step):
        m = lax.rem(t // 2 + step, TILES)
        blocks = []
        for b in range(2):
            block = 2 * m + b

            @pl.when(block != t)
            def _():
                bytes_of(own_in.at[block], own_rs.at[block])

            @pl.when((block != 0) & (block != t + 1))
            def _():
                bytes_of(spill_in.at[block], spill_rs.at[block])

            own = own_in[block].astype(F32)
            head = own[0:SPILL_ROWS] + spill_in[block].astype(F32)
            own = jnp.concatenate([head, own[SPILL_ROWS:]], axis=0).astype(BF16).astype(F32)
            blocks += [own[f * LOCAL : (f + 1) * LOCAL] for f in range(FRAMES)]
        for to, block in enumerate(butterfly(blocks, lane)):
            send1[m, to * LOCAL : (to + 1) * LOCAL, :] = block.astype(BF16)
        mine = pl.ds(pl.multiple_of(s * LOCAL, LOCAL), LOCAL)
        v[m, mine, :] = send1[m, mine, :]

        @pl.loop(1, STN)
        def _(d):
            turn_copy(m, lax.rem(s + d, STN)).start()

    def send_columns():
        bytes_of(ref_in.at[pl.ds(0, INPUTS - LOCAL)], ref_sem.at[3])
        row16 = lax.broadcasted_iota(jnp.int32, (2 * K, 1), 0)
        wanted = jnp.zeros((2 * K, 1), jnp.int32)
        for k in range(K):
            wanted = jnp.where(lax.rem(row16, K) == k, basis_in[k], wanted)
        column = lax.broadcasted_iota(jnp.int32, (2 * K, INPUTS), 1)
        onehot = jnp.where(column == wanted, 1.0, 0.0).astype(BF16)
        block = ref_in[...]
        picked = jnp.dot(onehot, block, preferred_element_type=F32)
        swapped = jnp.where((lane & 1) == 0, -pltpu.roll(picked, 127, 1), pltpu.roll(picked, 1, 1))
        left = jnp.where(row16 < K, picked, swapped)
        left = jnp.where(lane < 2 * FRAMES, left, 0.0).astype(BF16)
        columns = lax.dot_general(
            left, block, (((1,), (1,)), ((), ())), preferred_element_type=F32
        ).astype(BF16)
        cols_out[...] = columns
        cols_in[t] = columns

        @pl.loop(1, TM)
        def _(d):
            columns_copy(lax.rem(t + d, TM)).start()

    def find_basis():
        bytes_of(cols_in.at[pl.ds(0, TM - 1)], cols_sem.at[1])
        columns = cols_in[0].astype(F32)
        for other in range(1, TM):
            columns = columns + cols_in[other].astype(F32)
        columns = columns * (1.0 / SPECTRA)
        basis_re, basis_im = gram_schmidt(columns[0:K], columns[K:])
        basis[0:K, :] = basis_re
        basis[K:, :] = basis_im

    for step in range(TILES):
        turn(step)
        if step == COLUMNS_AT:
            send_columns()
    find_basis()

    low = basis[...].astype(BF16)
    rows16 = lax.broadcasted_iota(jnp.int32, (16, 128), 0)
    lanes16 = lax.broadcasted_iota(jnp.int32, (16, 128), 1)
    keep = (lanes16 // 64 == rows16 // 8) & (lax.rem(lanes16, 4) == 2 * lax.rem(rows16, 8))
    spectrum = jnp.where(
        lax.rem(lax.broadcasted_iota(jnp.int32, (128, 128), 0) // 4, FRAMES)
        == lax.broadcasted_iota(jnp.int32, (128, 128), 1),
        1.0,
        0.0,
    )
    for step in range(TILES):
        m = lax.rem(t // 2 + step, TILES)
        bytes_of(v.at[m, pl.ds(0, INPUTS - LOCAL)], rs1.at[m])
        z = jnp.dot(low, v[m], preferred_element_type=F32)
        z_re = z[0:K] + pltpu.roll(z[K:], 127, 1)
        z_im = pltpu.roll(z[0:K], 127, 1) - z[K:]
        squares = jnp.sum(z_re * z_re + z_im * z_im, axis=0, keepdims=True)
        both = jnp.dot(
            jnp.where(keep, squares, 0.0), spectrum, precision=HIGHEST, preferred_element_type=F32
        )
        pow_out[2 * m] = both[0:8]
        pow_out[2 * m + 1] = both[8:16]
    pow_in[t] = pow_out[t]

    @pl.loop(1, TM)
    def _(d):
        power_copy(lax.rem(t + d, TM)).start()

    covariances(v, basis, cov, proj)

    bytes_of(pow_in.at[pl.ds(0, TM - 1)], pow_rs)
    for owner in range(TM):
        power[2 * owner : 2 * owner + 2, :] = pow_in[owner, 0:2, 0:FRAMES]

    bytes_of(cols_in.at[pl.ds(0, TM - 1)], cols_sem.at[0])
    bytes_of(ref_in.at[pl.ds(0, INPUTS - LOCAL)], ref_sem.at[2])

    bytes_of(pow_out.at[pl.ds(0, TM - 1)], pow_ss)
    bytes_of(own_out.at[pl.ds(0, TM - 1)], own_ss)

    @pl.loop(0, TILES)
    def _(m):
        bytes_of(send1.at[m, pl.ds(0, INPUTS - LOCAL)], ss1.at[m])

    @pl.when(t < TM - 1)
    def _():
        bytes_of(ref_halo.at[0], ref_sem.at[0])
        bytes_of(spill_out.at[pl.ds(0, TM - 1)], spill_ss)


def channelise(volt, taps, table, ref_chan, basis_in):
    vmem = pl.BlockSpec(memory_space=pltpu.VMEM)
    hbm = pl.BlockSpec(memory_space=pltpu.HBM)
    dma = pltpu.SemaphoreType.DMA
    return pl.pallas_call(
        channelise_kernel,
        out_shape=(
            jax.ShapeDtypeStruct((2, INPUTS, 2 * INPUTS), BF16),
            jax.ShapeDtypeStruct((2, 2 * K * K), F32),
            jax.ShapeDtypeStruct((16, FRAMES), F32),
        ),
        in_specs=[hbm] * 5,
        out_specs=(vmem, vmem, vmem),
        scratch_shapes=[
            pltpu.VMEM((VOLT_ROWS, 128), jnp.int32),
            pltpu.VMEM((TAPS, NFFT), F32),
            pltpu.SMEM((1,), jnp.int32),
            pltpu.SMEM((K,), jnp.int32),
            pltpu.VMEM((PIECES, 2 * NFFT, 256), BF16),
            pltpu.VMEM((TAPS * Q, 128), F32),
            pltpu.VMEM((FRAMES * LOCAL * Q, 128), F32),
            pltpu.VMEM((FRAMES * LOCAL, 2 * NFFT), BF16),
            pltpu.VMEM((TM, SPILL_ROWS, 128), BF16),
            pltpu.VMEM((TM, SPILL_ROWS, 128), BF16),
            pltpu.VMEM((TM, OWN_ROWS, 128), BF16),
            pltpu.VMEM((TM, OWN_ROWS, 128), BF16),
            pltpu.VMEM((TILES, INPUTS, 128), BF16),
            pltpu.VMEM((2 * K, INPUTS), F32),
            pltpu.VMEM((TILES, INPUTS, 128), BF16),
            pltpu.VMEM((2, LOCAL, 128), BF16),
            pltpu.VMEM((LOCAL, 128), BF16),
            pltpu.VMEM((INPUTS, 128), BF16),
            pltpu.VMEM((2 * K, INPUTS), BF16),
            pltpu.VMEM((TM, 2 * K, INPUTS), BF16),
            pltpu.VMEM((TM, 8, 128), F32),
            pltpu.VMEM((TM, 8, 128), F32),
            dma((PARTS,)),
            dma((3,)),
            dma,
            dma,
            dma((TM,)),
            dma,
            dma((TM,)),
            dma((TILES,)),
            dma((TILES,)),
            dma((4,)),
            dma((2,)),
            dma,
            dma,
        ],
        compiler_params=pltpu.CompilerParams(
            collective_id=0, has_side_effects=True, vmem_limit_bytes=LIMIT * 1024 * 1024
        ),
        name="channelise",
    )(volt, taps, table, ref_chan, basis_in)


def write_kernel(cov_in, proj_in, power_in, cov, proj, power, sem):
    pieces = []
    for ch in range(2):
        for half in range(2):
            rows = pl.ds(half * (INPUTS // 2), INPUTS // 2)
            pieces.append(
                pltpu.make_async_copy(cov_in.at[ch, rows], cov.at[ch, rows], sem.at[ch * 2 + half])
            )
    for piece in pieces:
        piece.start()
    proj[...] = proj_in[...]
    power[...] = power_in[...]
    for piece in pieces:
        piece.wait()


def write(cov, proj, power):
    vmem = pl.BlockSpec(memory_space=pltpu.VMEM)
    whole = pl.BlockSpec(memory_space=pl.ANY)
    return pl.pallas_call(
        write_kernel,
        out_shape=tuple(jax.ShapeDtypeStruct(a.shape, a.dtype) for a in (cov, proj, power)),
        in_specs=[whole, vmem, vmem],
        out_specs=(whole, vmem, vmem),
        scratch_shapes=[pltpu.SemaphoreType.DMA((4,))],
        name="write",
    )(cov, proj, power)


FINAL = False


def on_device(table, voltages, filter_taps, reference_channel, basis_inputs):
    volt = voltages.reshape(LOCAL, 2, FRAMES * SUB, 128).transpose(0, 2, 1, 3).reshape(-1, 128)
    results = channelise(volt, filter_taps, table, reference_channel, basis_inputs)
    return write(*results) if FINAL else results


def solution(mesh):
    table = transform_table()

    def whole(voltages, filter_taps, reference_channel, basis_inputs):
        return jax.shard_map(
            on_device,
            mesh=mesh,
            in_specs=(P(), P("stn", None, "tm"), P(), P(), P()),
            out_specs=(P(("stn", "tm"), None, None), P(("stn", "tm"), None), P("stn", "tm")),
            check_vma=False,
        )(jnp.asarray(table), voltages, filter_taps, reference_channel, basis_inputs)

    return whole
```

```python
import functools
import math

import jax
import jax.numpy as jnp
import numpy as np
from jax import lax
from jax.experimental import pallas as pl
from jax.experimental.pallas import tpu as pltpu
from jax.sharding import PartitionSpec as P

NFFT = 1024
FCH = 512
TAPS = 16
K = 8
INPUTS = 512
SPECTRA = 128
STN = 32
TM = 8
LOCAL = INPUTS // STN
FRAMES = SPECTRA // TM
SUB = NFFT // 128
Q = 2 * SUB
SPILL = TAPS - 1
VOLT_ROWS = LOCAL * FRAMES * Q
COLUMNS_AT = 1
PARTS = 4
PIECES = 4
TILES = TM // 2
OWN_ROWS, SPILL_ROWS = FRAMES * LOCAL, SPILL * LOCAL
LIMIT = 56
MESH = pl.DeviceIdType.MESH
F32 = jnp.float32
BF16 = jnp.bfloat16
HIGHEST = lax.Precision.HIGHEST


def transform_table():
    phase = np.arange(NFFT)[:, None] * np.arange(FCH)[None, :] % NFFT
    angle = phase.astype(np.float32) * np.float32(2.0 * math.pi / NFFT)
    factor = np.float32(1.0 / math.sqrt(NFFT))
    cosine, sine = np.cos(angle) * factor, np.sin(angle) * factor
    table_re = np.stack([cosine, -sine], axis=2)
    table_im = np.stack([sine, cosine], axis=2)
    both = np.stack([table_re.reshape(SUB, 128, FCH, 2), table_im.reshape(SUB, 128, FCH, 2)], axis=1)
    both = both.reshape(2 * NFFT, STN, PIECES, 2, 2, 2)
    both = both.transpose(2, 0, 3, 1, 4, 5)
    return both.reshape(PIECES, 2 * NFFT, 256).astype(jnp.bfloat16)


def butterfly(blocks, lane):
    blocks = list(blocks)
    for bit in range(5):
        step, shift = 1 << bit, 4 << bit
        low = (lane & shift) == 0
        for a in range(32):
            if a & step:
                continue
            first, second = blocks[a], blocks[a | step]
            blocks[a] = jnp.where(low, first, pltpu.roll(second, shift, 1))
            blocks[a | step] = jnp.where(low, pltpu.roll(first, 128 - shift, 1), second)
    return blocks


def gram_schmidt(vec_re, vec_im):
    row = lax.broadcasted_iota(jnp.int32, (K, 1), 0)
    for k in range(K):
        w_re, w_im = vec_re[k : k + 1], vec_im[k : k + 1]
        in_re = jnp.sum(w_re * vec_re + w_im * vec_im, axis=1, keepdims=True)
        in_im = jnp.sum(w_re * vec_im - w_im * vec_re, axis=1, keepdims=True)
        inverse = lax.rsqrt(in_re[k : k + 1] + 1e-06)
        q_re, q_im = w_re * inverse, w_im * inverse
        c_re = jnp.where(row > k, in_re * inverse, 0.0)
        c_im = jnp.where(row > k, in_im * inverse, 0.0)
        new_re = vec_re - (q_re * c_re - q_im * c_im)
        new_im = vec_im - (q_re * c_im + q_im * c_re)
        vec_re = jnp.where(row == k, q_re, new_re)
        vec_im = jnp.where(row == k, q_im, new_im)
    return vec_re, vec_im


def covariances(v, basis, cov, proj, done):
    lane4 = lax.broadcasted_iota(jnp.int32, (1, 512), 1)
    x = jnp.concatenate([v[m].astype(F32) for m in range(TILES)], axis=1)
    real = (lane4 & 1) == 0
    swapped = jnp.where(real, pltpu.roll(x, 511, 1), -pltpu.roll(x, 1, 1))
    x_low, swapped = x.astype(BF16), swapped.astype(BF16)
    for ch in range(2):
        keep = (lane4 & 2) == 2 * ch
        for part, left in enumerate((x_low, swapped)):
            left = jnp.where(keep, left, jnp.zeros_like(left))
            prod = lax.dot_general(
                left, x_low, (((1,), (1,)), ((), ())), preferred_element_type=F32
            )
            cov[ch, :, part * INPUTS : (part + 1) * INPUTS] = (prod * (1.0 / SPECTRA)).astype(BF16)
        done(ch)

    b = basis[...]
    b0 = b.astype(BF16)
    rest = b - b0.astype(F32)
    b1 = rest.astype(BF16)
    b2 = (rest - b1.astype(F32)).astype(BF16)
    y = sum(jnp.dot(part, x_low, preferred_element_type=F32) for part in (b2, b1, b0))
    y_re = y[0:K] + pltpu.roll(y[K:], 511, 1)
    y_im = pltpu.roll(y[0:K], 511, 1) - y[K:]
    y = jnp.concatenate([y_re, y_im], axis=0)
    row = lax.broadcasted_iota(jnp.int32, (K, 128), 0)
    col = lax.broadcasted_iota(jnp.int32, (K, 128), 1)
    for ch in range(2):
        left = jnp.where((lane4 & 3) == 2 * ch, y, 0.0)
        gram = lax.dot_general(
            left, y, (((1,), (1,)), ((), ())), precision=HIGHEST, preferred_element_type=F32
        )
        re = gram[0:K, 0:K] + gram[K:, K:]
        im = gram[K:, 0:K] - gram[0:K, K:]
        flat = jnp.concatenate([re] * K + [im] * K, axis=1)
        flat = jnp.where(lax.rem(col // K, K) == row, flat, 0.0)
        proj[ch : ch + 1, :] = jnp.sum(flat, axis=0, keepdims=True) * (1.0 / SPECTRA)


def channelise_kernel(
    volt_hbm, taps_hbm, table_hbm, ref_hbm, basis_hbm,
    cov, proj, power,
    volt, taps, ref_chan, basis_in, table, tap_rows, frames_f, lhs, spill_out, spill_in, own_out, own_in,
    v, basis, send1, ref_halo, ref_out, ref_in, cols_out, cols_in, pow_out, pow_in,
    volt_sem, small_sem, table_sem, spill_ss, spill_rs, own_ss, own_rs, ss1, rs1, ref_sem, cols_sem, pow_ss, pow_rs,
):
    s = lax.axis_index("stn")
    t = lax.axis_index("tm")
    load_taps = pltpu.make_async_copy(taps_hbm, taps, small_sem.at[0])
    load_taps.start()
    load_ref = pltpu.make_async_copy(ref_hbm, ref_chan, small_sem.at[1])
    load_ref.start()
    load_basis = pltpu.make_async_copy(basis_hbm, basis_in, small_sem.at[2])
    load_basis.start()

    def load_volt(part):
        rows = pl.ds(pl.multiple_of(part * (VOLT_ROWS // PARTS), 8), VOLT_ROWS // PARTS)
        return pltpu.make_async_copy(volt_hbm.at[rows], volt.at[rows], volt_sem.at[part])

    for part in range(PARTS):
        load_volt(part).start()
    load_table = pltpu.make_async_copy(table_hbm, table, table_sem)
    load_table.start()

    barrier = pltpu.get_barrier_semaphore()

    @pl.loop(1, STN)
    def _(d):
        pl.semaphore_signal(barrier, 1, device_id={"stn": lax.rem(s + d, STN)}, device_id_type=MESH)

    @pl.loop(1, TM)
    def _(d):
        pl.semaphore_signal(barrier, 1, device_id={"tm": lax.rem(t + d, TM)}, device_id_type=MESH)

    load_taps.wait()
    for sub in range(SUB):
        part = taps[:, sub * 128 : (sub + 1) * 128] * (1.0 / 64.0)
        for p in range(2):
            tap_rows[pl.ds(sub * 2 + p, TAPS, stride=Q), :] = part

    def filter_frames(spill):
        @pl.loop(0, LOCAL * 2)
        def _(step):
            if spill:
                @pl.when(lax.rem(step, LOCAL * 2 // PARTS) == 0)
                def _():
                    load_volt(step // (LOCAL * 2 // PARTS)).wait()

            i, half = step // 2, lax.rem(step, 2)
            base = pl.multiple_of(i * (FRAMES * Q) + half * 8, 8)
            x = [volt[pl.ds(base + f * Q, 8), :].astype(F32) for f in range(FRAMES)]
            tap = [tap_rows[pl.ds(pl.multiple_of(k * Q + half * 8, 8), 8), :] for k in range(TAPS)]
            for f in range(SPILL if spill else FRAMES):
                acc = None
                for j in range(f + 1, FRAMES) if spill else range(f + 1):
                    k = j - f - 1 if spill else SPILL - f + j
                    term = tap[k] * x[j]
                    acc = term if acc is None else acc + term
                row = pl.multiple_of((f * LOCAL + i) * Q + half * 8, 8)
                frames_f[pl.ds(row, 8), :] = acc

        rows = (SPILL if spill else FRAMES) * LOCAL
        for q in range(Q):
            lhs[0:rows, q * 128 : (q + 1) * 128] = frames_f[pl.ds(q, rows, stride=Q), :].astype(BF16)

    def spill_copy(to):
        return pltpu.make_async_remote_copy(
            src_ref=spill_out.at[to],
            dst_ref=spill_in.at[lax.rem(t + 1, TM)],
            send_sem=spill_ss,
            recv_sem=spill_rs.at[lax.rem(t + 1, TM)],
            device_id={"tm": to},
            device_id_type=MESH,
        )

    def own_copy(to):
        return pltpu.make_async_remote_copy(
            src_ref=own_out.at[to],
            dst_ref=own_in.at[t],
            send_sem=own_ss,
            recv_sem=own_rs.at[t],
            device_id={"tm": to},
            device_id_type=MESH,
        )

    def turn_copy(m, to):
        return pltpu.make_async_remote_copy(
            src_ref=send1.at[m, pl.ds(pl.multiple_of(to * LOCAL, LOCAL), LOCAL)],
            dst_ref=v.at[m, pl.ds(pl.multiple_of(s * LOCAL, LOCAL), LOCAL)],
            send_sem=ss1.at[m],
            recv_sem=rs1.at[m],
            device_id={"stn": to},
            device_id_type=MESH,
        )

    def power_copy(to):
        return pltpu.make_async_remote_copy(
            src_ref=pow_out.at[to],
            dst_ref=pow_in.at[t],
            send_sem=pow_ss,
            recv_sem=pow_rs,
            device_id={"tm": to},
            device_id_type=MESH,
        )

    def bytes_of(ref, sem):
        pltpu.make_async_copy(ref, ref, sem).wait()

    lane = lax.broadcasted_iota(jnp.int32, (1, 128), 1)

    def ref_tile(rows, ref_table):
        part = jnp.dot(lhs[0 : rows * LOCAL, :], ref_table, preferred_element_type=F32)
        total = jnp.zeros((LOCAL, 128), F32)
        for f in range(rows):
            total = total + jnp.where(
                lax.rem(lane // 2, FRAMES) == f, part[f * LOCAL : (f + 1) * LOCAL], 0.0
            )
        return total

    def ref_halo_copy():
        return pltpu.make_async_remote_copy(
            src_ref=ref_halo.at[0],
            dst_ref=ref_halo.at[1],
            send_sem=ref_sem.at[0],
            recv_sem=ref_sem.at[1],
            device_id={"tm": lax.rem(t + 1, TM)},
            device_id_type=MESH,
        )

    def ref_copy(to):
        return pltpu.make_async_remote_copy(
            src_ref=ref_out,
            dst_ref=ref_in.at[pl.ds(pl.multiple_of(s * LOCAL, LOCAL), LOCAL)],
            send_sem=ref_sem.at[2],
            recv_sem=ref_sem.at[3],
            device_id={"stn": to},
            device_id_type=MESH,
        )

    def columns_copy(to):
        return pltpu.make_async_remote_copy(
            src_ref=cols_out,
            dst_ref=cols_in.at[t],
            send_sem=cols_sem.at[0],
            recv_sem=cols_sem.at[1],
            device_id={"tm": to},
            device_id_type=MESH,
        )

    filter_frames(True)
    load_table.wait()
    load_ref.wait()
    load_basis.wait()
    ref = ref_chan[0]
    ref_stn, ref_tm, ref_low = ref // 16, lax.rem(ref // 2, TM), lax.rem(ref, 2)
    ref_at = lax.rem(ref_tm, 2) * 128 + ref_stn * 4 + ref_low * 2
    chosen = lax.broadcasted_iota(jnp.int32, (256, 128), 0) == ref_at + (lane & 1)
    ref_table = jnp.dot(
        table[ref_tm // 2],
        jnp.where(chosen, 1.0, 0.0).astype(BF16),
        preferred_element_type=F32,
    ).astype(BF16)
    ref_halo[0] = ref_tile(SPILL, ref_table).astype(BF16)
    for piece in range(PIECES):
        part = jnp.dot(lhs[0:SPILL_ROWS, :], table[piece], preferred_element_type=F32).astype(BF16)
        spill_out[2 * piece] = part[:, 0:128]
        spill_out[2 * piece + 1] = part[:, 128:]

    @pl.when(t < TM - 1)
    def _():
        spill_in[t + 1] = spill_out[t]

    spill_in[0] = jnp.zeros((SPILL_ROWS, 128), BF16)

    pl.semaphore_wait(barrier, STN - 1 + TM - 1)

    @pl.when(t < TM - 1)
    def _():
        ref_halo_copy().start()

        @pl.loop(1, TM)
        def _(d):
            spill_copy(lax.rem(t + d, TM)).start()

    filter_frames(False)

    for step in range(PIECES):
        piece = lax.rem(t // 2 + 1 + step, PIECES)
        part = jnp.dot(lhs[...], table[piece], preferred_element_type=F32).astype(BF16)
        for b in range(2):
            to = 2 * piece + b
            own_out[to] = part[:, b * 128 : (b + 1) * 128]

            @pl.when(to != t)
            def _():
                own_copy(to).start()

    own_in[t] = own_out[t]

    @pl.when(t == 0)
    def _():
        ref_halo[1] = jnp.zeros((LOCAL, 128), BF16)

    own_ref = ref_tile(FRAMES, ref_table)

    @pl.when(t > 0)
    def _():
        bytes_of(ref_halo.at[1], ref_sem.at[1])

    ref_out[...] = (own_ref + ref_halo[1].astype(F32)).astype(BF16)
    ref_in[pl.ds(pl.multiple_of(s * LOCAL, LOCAL), LOCAL), :] = ref_out[...]

    @pl.loop(1, STN)
    def _(d):
        ref_copy(lax.rem(s + d, STN)).start()

    def turn(step):
        m = lax.rem(t // 2 + step, TILES)
        blocks = []
        for b in range(2):
            block = 2 * m + b

            @pl.when(block != t)
            def _():
                bytes_of(own_in.at[block], own_rs.at[block])

            @pl.when((block != 0) & (block != t + 1))
            def _():
                bytes_of(spill_in.at[block], spill_rs.at[block])

            own = own_in[block].astype(F32)
            head = own[0:SPILL_ROWS] + spill_in[block].astype(F32)
            own = jnp.concatenate([head, own[SPILL_ROWS:]], axis=0).astype(BF16).astype(F32)
            blocks += [own[f * LOCAL : (f + 1) * LOCAL] for f in range(FRAMES)]
        for to, block in enumerate(butterfly(blocks, lane)):
            send1[m, to * LOCAL : (to + 1) * LOCAL, :] = block.astype(BF16)
        mine = pl.ds(pl.multiple_of(s * LOCAL, LOCAL), LOCAL)
        v[m, mine, :] = send1[m, mine, :]

        @pl.loop(1, STN)
        def _(d):
            turn_copy(m, lax.rem(s + d, STN)).start()

    def send_columns():
        bytes_of(ref_in.at[pl.ds(0, INPUTS - LOCAL)], ref_sem.at[3])
        row16 = lax.broadcasted_iota(jnp.int32, (2 * K, 1), 0)
        wanted = jnp.zeros((2 * K, 1), jnp.int32)
        for k in range(K):
            wanted = jnp.where(lax.rem(row16, K) == k, basis_in[k], wanted)
        column = lax.broadcasted_iota(jnp.int32, (2 * K, INPUTS), 1)
        onehot = jnp.where(column == wanted, 1.0, 0.0).astype(BF16)
        block = ref_in[...]
        picked = jnp.dot(onehot, block, preferred_element_type=F32)
        swapped = jnp.where((lane & 1) == 0, -pltpu.roll(picked, 127, 1), pltpu.roll(picked, 1, 1))
        left = jnp.where(row16 < K, picked, swapped)
        left = jnp.where(lane < 2 * FRAMES, left, 0.0).astype(BF16)
        columns = lax.dot_general(
            left, block, (((1,), (1,)), ((), ())), preferred_element_type=F32
        ).astype(BF16)
        cols_out[...] = columns
        cols_in[t] = columns

        @pl.loop(1, TM)
        def _(d):
            columns_copy(lax.rem(t + d, TM)).start()

    def find_basis():
        bytes_of(cols_in.at[pl.ds(0, TM - 1)], cols_sem.at[1])
        columns = cols_in[0].astype(F32)
        for other in range(1, TM):
            columns = columns + cols_in[other].astype(F32)
        columns = columns * (1.0 / SPECTRA)
        basis_re, basis_im = gram_schmidt(columns[0:K], columns[K:])
        basis[0:K, :] = basis_re
        basis[K:, :] = basis_im

    for step in range(TILES):
        turn(step)
        if step == COLUMNS_AT:
            send_columns()
    find_basis()

    low = basis[...].astype(BF16)
    rows16 = lax.broadcasted_iota(jnp.int32, (16, 128), 0)
    lanes16 = lax.broadcasted_iota(jnp.int32, (16, 128), 1)
    keep = (lanes16 // 64 == rows16 // 8) & (lax.rem(lanes16, 4) == 2 * lax.rem(rows16, 8))
    spectrum = jnp.where(
        lax.rem(lax.broadcasted_iota(jnp.int32, (128, 128), 0) // 4, FRAMES)
        == lax.broadcasted_iota(jnp.int32, (128, 128), 1),
        1.0,
        0.0,
    )
    for step in range(TILES):
        m = lax.rem(t // 2 + step, TILES)
        bytes_of(v.at[m, pl.ds(0, INPUTS - LOCAL)], rs1.at[m])
        z = jnp.dot(low, v[m], preferred_element_type=F32)
        z_re = z[0:K] + pltpu.roll(z[K:], 127, 1)
        z_im = pltpu.roll(z[0:K], 127, 1) - z[K:]
        squares = jnp.sum(z_re * z_re + z_im * z_im, axis=0, keepdims=True)
        both = jnp.dot(
            jnp.where(keep, squares, 0.0), spectrum, precision=HIGHEST, preferred_element_type=F32
        )
        pow_out[2 * m] = both[0:8]
        pow_out[2 * m + 1] = both[8:16]
    pow_in[t] = pow_out[t]

    @pl.loop(1, TM)
    def _(d):
        power_copy(lax.rem(t + d, TM)).start()

    covariances(v, basis, cov, proj, lambda ch: None)

    bytes_of(pow_in.at[pl.ds(0, TM - 1)], pow_rs)
    for owner in range(TM):
        power[2 * owner : 2 * owner + 2, :] = pow_in[owner, 0:2, 0:FRAMES]

    bytes_of(cols_in.at[pl.ds(0, TM - 1)], cols_sem.at[0])
    bytes_of(ref_in.at[pl.ds(0, INPUTS - LOCAL)], ref_sem.at[2])

    bytes_of(pow_out.at[pl.ds(0, TM - 1)], pow_ss)
    bytes_of(own_out.at[pl.ds(0, TM - 1)], own_ss)

    @pl.loop(0, TILES)
    def _(m):
        bytes_of(send1.at[m, pl.ds(0, INPUTS - LOCAL)], ss1.at[m])

    @pl.when(t < TM - 1)
    def _():
        bytes_of(ref_halo.at[0], ref_sem.at[0])
        bytes_of(spill_out.at[pl.ds(0, TM - 1)], spill_ss)


def channelise(volt, taps, table, ref_chan, basis_in):
    vmem = pl.BlockSpec(memory_space=pltpu.VMEM)
    hbm = pl.BlockSpec(memory_space=pltpu.HBM)
    dma = pltpu.SemaphoreType.DMA
    return pl.pallas_call(
        channelise_kernel,
        out_shape=(
            pltpu.VMEM((2, INPUTS, 2 * INPUTS), BF16),
            pltpu.VMEM((2, 2 * K * K), F32),
            pltpu.VMEM((16, FRAMES), F32),
        ),
        in_specs=[hbm] * 5,
        out_specs=(vmem, vmem, vmem),
        scratch_shapes=[
            pltpu.VMEM((VOLT_ROWS, 128), jnp.int32),
            pltpu.VMEM((TAPS, NFFT), F32),
            pltpu.SMEM((1,), jnp.int32),
            pltpu.SMEM((K,), jnp.int32),
            pltpu.VMEM((PIECES, 2 * NFFT, 256), BF16),
            pltpu.VMEM((TAPS * Q, 128), F32),
            pltpu.VMEM((FRAMES * LOCAL * Q, 128), F32),
            pltpu.VMEM((FRAMES * LOCAL, 2 * NFFT), BF16),
            pltpu.VMEM((TM, SPILL_ROWS, 128), BF16),
            pltpu.VMEM((TM, SPILL_ROWS, 128), BF16),
            pltpu.VMEM((TM, OWN_ROWS, 128), BF16),
            pltpu.VMEM((TM, OWN_ROWS, 128), BF16),
            pltpu.VMEM((TILES, INPUTS, 128), BF16),
            pltpu.VMEM((2 * K, INPUTS), F32),
            pltpu.VMEM((TILES, INPUTS, 128), BF16),
            pltpu.VMEM((2, LOCAL, 128), BF16),
            pltpu.VMEM((LOCAL, 128), BF16),
            pltpu.VMEM((INPUTS, 128), BF16),
            pltpu.VMEM((2 * K, INPUTS), BF16),
            pltpu.VMEM((TM, 2 * K, INPUTS), BF16),
            pltpu.VMEM((TM, 8, 128), F32),
            pltpu.VMEM((TM, 8, 128), F32),
            dma((PARTS,)),
            dma((3,)),
            dma,
            dma,
            dma((TM,)),
            dma,
            dma((TM,)),
            dma((TILES,)),
            dma((TILES,)),
            dma((4,)),
            dma((2,)),
            dma,
            dma,
        ],
        compiler_params=pltpu.CompilerParams(
            collective_id=0, has_side_effects=True, vmem_limit_bytes=LIMIT * 1024 * 1024
        ),
        name="channelise",
    )(volt, taps, table, ref_chan, basis_in)


def write_kernel(cov_in, proj_in, power_in, cov, proj, power, sem):
    def store(p):
        rows = pl.ds(p % 2 * (INPUTS // 2), INPUTS // 2)
        return pltpu.make_async_copy(cov_in.at[p // 2, rows], cov.at[p // 2, rows], sem.at[p])

    for p in range(4):
        store(p).start()
    proj[...] = proj_in[...]
    power[...] = power_in[...]
    for p in range(4):
        store(p).wait()


def write(cov, proj, power):
    vmem = pl.BlockSpec(memory_space=pltpu.VMEM)
    hbm = pl.BlockSpec(memory_space=pltpu.HBM)
    return pl.pallas_call(
        write_kernel,
        out_shape=tuple(jax.ShapeDtypeStruct(a.shape, a.dtype) for a in (cov, proj, power)),
        in_specs=[vmem, vmem, vmem],
        out_specs=(hbm, vmem, vmem),
        scratch_shapes=[pltpu.SemaphoreType.DMA((4,))],
        compiler_params=pltpu.CompilerParams(vmem_limit_bytes=16 * 1024 * 1024),
        name="write",
    )(cov, proj, power)


def on_device(table, voltages, filter_taps, reference_channel, basis_inputs):
    volt = voltages.reshape(LOCAL, 2, FRAMES * SUB, 128).transpose(0, 2, 1, 3).reshape(-1, 128)
    volt = pltpu.with_memory_space_constraint(volt, pltpu.HBM)
    table = pltpu.with_memory_space_constraint(table, pltpu.HBM)
    results = channelise(volt, filter_taps, table, reference_channel, basis_inputs)
    return write(*results)


def solution(mesh):
    table = transform_table()

    def whole(voltages, filter_taps, reference_channel, basis_inputs):
        return jax.shard_map(
            on_device,
            mesh=mesh,
            in_specs=(P(), P("stn", None, "tm"), P(), P(), P()),
            out_specs=(P(("stn", "tm"), None, None), P(("stn", "tm"), None), P("stn", "tm")),
            check_vma=False,
        )(jnp.asarray(table), voltages, filter_taps, reference_channel, basis_inputs)

    return whole
```

```python
import functools
import math

import jax
import jax.numpy as jnp
import numpy as np
from jax import lax
from jax.experimental import pallas as pl
from jax.experimental.pallas import tpu as pltpu
from jax.sharding import PartitionSpec as P

NFFT = 1024
FCH = 512
TAPS = 16
K = 8
INPUTS = 512
SPECTRA = 128
STN = 32
TM = 8
LOCAL = INPUTS // STN
FRAMES = SPECTRA // TM
SUB = NFFT // 128
Q = 2 * SUB
SPILL = TAPS - 1
VOLT_ROWS = LOCAL * FRAMES * Q
COLUMNS_AT = 1
PARTS = 4
PIECES = 4
TILES = TM // 2
OWN_ROWS, SPILL_ROWS = FRAMES * LOCAL, SPILL * LOCAL
LIMIT = 56
MESH = pl.DeviceIdType.MESH
F32 = jnp.float32
BF16 = jnp.bfloat16
HIGHEST = lax.Precision.HIGHEST


def transform_table():
    phase = np.arange(NFFT)[:, None] * np.arange(FCH)[None, :] % NFFT
    angle = phase.astype(np.float32) * np.float32(2.0 * math.pi / NFFT)
    factor = np.float32(1.0 / math.sqrt(NFFT))
    cosine, sine = np.cos(angle) * factor, np.sin(angle) * factor
    table_re = np.stack([cosine, -sine], axis=2)
    table_im = np.stack([sine, cosine], axis=2)
    both = np.stack([table_re.reshape(SUB, 128, FCH, 2), table_im.reshape(SUB, 128, FCH, 2)], axis=1)
    both = both.reshape(2 * NFFT, STN, PIECES, 2, 2, 2)
    both = both.transpose(2, 0, 3, 1, 4, 5)
    return both.reshape(PIECES, 2 * NFFT, 256).astype(jnp.bfloat16)


def butterfly(blocks, lane):
    blocks = list(blocks)
    for bit in range(5):
        step, shift = 1 << bit, 4 << bit
        low = (lane & shift) == 0
        for a in range(32):
            if a & step:
                continue
            first, second = blocks[a], blocks[a | step]
            blocks[a] = jnp.where(low, first, pltpu.roll(second, shift, 1))
            blocks[a | step] = jnp.where(low, pltpu.roll(first, 128 - shift, 1), second)
    return blocks


def gram_schmidt(vec_re, vec_im):
    row = lax.broadcasted_iota(jnp.int32, (K, 1), 0)
    for k in range(K):
        w_re, w_im = vec_re[k : k + 1], vec_im[k : k + 1]
        in_re = jnp.sum(w_re * vec_re + w_im * vec_im, axis=1, keepdims=True)
        in_im = jnp.sum(w_re * vec_im - w_im * vec_re, axis=1, keepdims=True)
        inverse = lax.rsqrt(in_re[k : k + 1] + 1e-06)
        q_re, q_im = w_re * inverse, w_im * inverse
        c_re = jnp.where(row > k, in_re * inverse, 0.0)
        c_im = jnp.where(row > k, in_im * inverse, 0.0)
        new_re = vec_re - (q_re * c_re - q_im * c_im)
        new_im = vec_im - (q_re * c_im + q_im * c_re)
        vec_re = jnp.where(row == k, q_re, new_re)
        vec_im = jnp.where(row == k, q_im, new_im)
    return vec_re, vec_im


def covariances(v, basis, cov, proj, done):
    lane4 = lax.broadcasted_iota(jnp.int32, (1, 512), 1)
    x = jnp.concatenate([v[m].astype(F32) for m in range(TILES)], axis=1)
    real = (lane4 & 1) == 0
    swapped = jnp.where(real, pltpu.roll(x, 511, 1), -pltpu.roll(x, 1, 1))
    x_low, swapped = x.astype(BF16), swapped.astype(BF16)
    for ch in range(2):
        keep = (lane4 & 2) == 2 * ch
        for part, left in enumerate((x_low, swapped)):
            left = jnp.where(keep, left, jnp.zeros_like(left))
            prod = lax.dot_general(
                left, x_low, (((1,), (1,)), ((), ())), preferred_element_type=F32
            )
            cov[ch, :, part * INPUTS : (part + 1) * INPUTS] = (prod * (1.0 / SPECTRA)).astype(BF16)
        done(ch)

    b = basis[...]
    b0 = b.astype(BF16)
    rest = b - b0.astype(F32)
    b1 = rest.astype(BF16)
    b2 = (rest - b1.astype(F32)).astype(BF16)
    y = sum(jnp.dot(part, x_low, preferred_element_type=F32) for part in (b2, b1, b0))
    y_re = y[0:K] + pltpu.roll(y[K:], 511, 1)
    y_im = pltpu.roll(y[0:K], 511, 1) - y[K:]
    y = jnp.concatenate([y_re, y_im], axis=0)
    row = lax.broadcasted_iota(jnp.int32, (K, 128), 0)
    col = lax.broadcasted_iota(jnp.int32, (K, 128), 1)
    for ch in range(2):
        left = jnp.where((lane4 & 3) == 2 * ch, y, 0.0)
        gram = lax.dot_general(
            left, y, (((1,), (1,)), ((), ())), precision=HIGHEST, preferred_element_type=F32
        )
        re = gram[0:K, 0:K] + gram[K:, K:]
        im = gram[K:, 0:K] - gram[0:K, K:]
        flat = jnp.concatenate([re] * K + [im] * K, axis=1)
        flat = jnp.where(lax.rem(col // K, K) == row, flat, 0.0)
        proj[ch : ch + 1, :] = jnp.sum(flat, axis=0, keepdims=True) * (1.0 / SPECTRA)


def channelise_kernel(
    volt_hbm, taps_hbm, table_hbm, ref_hbm, basis_hbm,
    cov, proj, power,
    volt, taps, ref_chan, basis_in, table, tap_rows, frames_f, lhs, spill_out, spill_in, own_out, own_in,
    v, basis, send1, ref_halo, ref_out, ref_near, ref_pack, ref_in, cols_out, cols_in, pow_out, pow_in,
    volt_sem, small_sem, table_sem, spill_ss, spill_rs, own_ss, own_rs, ss1, rs1, ref_sem, cols_sem, pow_ss, pow_rs,
):
    s = lax.axis_index("stn")
    t = lax.axis_index("tm")
    load_taps = pltpu.make_async_copy(taps_hbm, taps, small_sem.at[0])
    load_taps.start()
    load_ref = pltpu.make_async_copy(ref_hbm, ref_chan, small_sem.at[1])
    load_ref.start()
    load_basis = pltpu.make_async_copy(basis_hbm, basis_in, small_sem.at[2])
    load_basis.start()

    def load_volt(part):
        rows = pl.ds(pl.multiple_of(part * (VOLT_ROWS // PARTS), 8), VOLT_ROWS // PARTS)
        return pltpu.make_async_copy(volt_hbm.at[rows], volt.at[rows], volt_sem.at[part])

    for part in range(PARTS):
        load_volt(part).start()
    load_table = pltpu.make_async_copy(table_hbm, table, table_sem)
    load_table.start()

    barrier = pltpu.get_barrier_semaphore()

    @pl.loop(1, STN)
    def _(d):
        pl.semaphore_signal(barrier, 1, device_id={"stn": lax.rem(s + d, STN)}, device_id_type=MESH)

    @pl.loop(1, TM)
    def _(d):
        pl.semaphore_signal(barrier, 1, device_id={"tm": lax.rem(t + d, TM)}, device_id_type=MESH)

    load_taps.wait()
    for sub in range(SUB):
        part = taps[:, sub * 128 : (sub + 1) * 128] * (1.0 / 64.0)
        for p in range(2):
            tap_rows[pl.ds(sub * 2 + p, TAPS, stride=Q), :] = part

    def filter_frames(spill):
        @pl.loop(0, LOCAL * 2)
        def _(step):
            if spill:
                @pl.when(lax.rem(step, LOCAL * 2 // PARTS) == 0)
                def _():
                    load_volt(step // (LOCAL * 2 // PARTS)).wait()

            i, half = step // 2, lax.rem(step, 2)
            base = pl.multiple_of(i * (FRAMES * Q) + half * 8, 8)
            x = [volt[pl.ds(base + f * Q, 8), :].astype(F32) for f in range(FRAMES)]
            tap = [tap_rows[pl.ds(pl.multiple_of(k * Q + half * 8, 8), 8), :] for k in range(TAPS)]
            for f in range(SPILL if spill else FRAMES):
                acc = None
                for j in range(f + 1, FRAMES) if spill else range(f + 1):
                    k = j - f - 1 if spill else SPILL - f + j
                    term = tap[k] * x[j]
                    acc = term if acc is None else acc + term
                row = pl.multiple_of((f * LOCAL + i) * Q + half * 8, 8)
                frames_f[pl.ds(row, 8), :] = acc

        rows = (SPILL if spill else FRAMES) * LOCAL
        for q in range(Q):
            lhs[0:rows, q * 128 : (q + 1) * 128] = frames_f[pl.ds(q, rows, stride=Q), :].astype(BF16)

    def spill_copy(to):
        return pltpu.make_async_remote_copy(
            src_ref=spill_out.at[to],
            dst_ref=spill_in.at[lax.rem(t + 1, TM)],
            send_sem=spill_ss,
            recv_sem=spill_rs.at[lax.rem(t + 1, TM)],
            device_id={"tm": to},
            device_id_type=MESH,
        )

    def own_copy(to):
        return pltpu.make_async_remote_copy(
            src_ref=own_out.at[to],
            dst_ref=own_in.at[t],
            send_sem=own_ss,
            recv_sem=own_rs.at[t],
            device_id={"tm": to},
            device_id_type=MESH,
        )

    def turn_copy(m, to):
        return pltpu.make_async_remote_copy(
            src_ref=send1.at[m, pl.ds(pl.multiple_of(to * LOCAL, LOCAL), LOCAL)],
            dst_ref=v.at[m, pl.ds(pl.multiple_of(s * LOCAL, LOCAL), LOCAL)],
            send_sem=ss1.at[m],
            recv_sem=rs1.at[m],
            device_id={"stn": to},
            device_id_type=MESH,
        )

    def power_copy(to):
        return pltpu.make_async_remote_copy(
            src_ref=pow_out.at[to],
            dst_ref=pow_in.at[t],
            send_sem=pow_ss,
            recv_sem=pow_rs,
            device_id={"tm": to},
            device_id_type=MESH,
        )

    def bytes_of(ref, sem):
        pltpu.make_async_copy(ref, ref, sem).wait()

    lane = lax.broadcasted_iota(jnp.int32, (1, 128), 1)

    def ref_tile(rows, ref_table):
        part = jnp.dot(lhs[0 : rows * LOCAL, :], ref_table, preferred_element_type=F32)
        total = jnp.zeros((LOCAL, 128), F32)
        for f in range(rows):
            total = total + jnp.where(
                lax.rem(lane // 2, FRAMES) == f, part[f * LOCAL : (f + 1) * LOCAL], 0.0
            )
        return total

    def ref_halo_copy():
        return pltpu.make_async_remote_copy(
            src_ref=ref_halo.at[0],
            dst_ref=ref_halo.at[1],
            send_sem=ref_sem.at[0],
            recv_sem=ref_sem.at[1],
            device_id={"tm": lax.rem(t + 1, TM)},
            device_id_type=MESH,
        )

    y, z, core = s // 8, lax.rem(s // 2, 4), lax.rem(s, 2)

    def near_copy(d):
        to = lax.rem(y * 2 + core + d, 8)
        return pltpu.make_async_remote_copy(
            src_ref=ref_out,
            dst_ref=ref_near.at[core * 4 + y],
            send_sem=ref_sem.at[2],
            recv_sem=ref_sem.at[3],
            device_id={"stn": to // 2 * 8 + z * 2 + lax.rem(to, 2)},
            device_id_type=MESH,
        )

    def far_copy(d):
        return pltpu.make_async_remote_copy(
            src_ref=ref_pack,
            dst_ref=ref_in.at[pl.ds(pl.multiple_of(z * 2 * LOCAL, 2 * LOCAL), 2 * LOCAL)],
            send_sem=ref_sem.at[4],
            recv_sem=ref_sem.at[5],
            device_id={"stn": y * 8 + lax.rem(z + d, 4) * 2 + core},
            device_id_type=MESH,
        )

    def columns_copy(to):
        return pltpu.make_async_remote_copy(
            src_ref=cols_out,
            dst_ref=cols_in.at[t],
            send_sem=cols_sem.at[0],
            recv_sem=cols_sem.at[1],
            device_id={"tm": to},
            device_id_type=MESH,
        )

    filter_frames(True)
    load_table.wait()
    load_ref.wait()
    load_basis.wait()
    ref = ref_chan[0]
    ref_stn, ref_tm, ref_low = ref // 16, lax.rem(ref // 2, TM), lax.rem(ref, 2)
    ref_at = lax.rem(ref_tm, 2) * 128 + ref_stn * 4 + ref_low * 2
    chosen = lax.broadcasted_iota(jnp.int32, (256, 128), 0) == ref_at + (lane & 1)
    ref_table = jnp.dot(
        table[ref_tm // 2],
        jnp.where(chosen, 1.0, 0.0).astype(BF16),
        preferred_element_type=F32,
    ).astype(BF16)
    ref_halo[0] = ref_tile(SPILL, ref_table).astype(BF16)
    for piece in range(PIECES):
        part = jnp.dot(lhs[0:SPILL_ROWS, :], table[piece], preferred_element_type=F32).astype(BF16)
        spill_out[2 * piece] = part[:, 0:128]
        spill_out[2 * piece + 1] = part[:, 128:]

    @pl.when(t < TM - 1)
    def _():
        spill_in[t + 1] = spill_out[t]

    spill_in[0] = jnp.zeros((SPILL_ROWS, 128), BF16)

    pl.semaphore_wait(barrier, STN - 1 + TM - 1)

    @pl.when(t < TM - 1)
    def _():
        ref_halo_copy().start()

        @pl.loop(1, TM)
        def _(d):
            spill_copy(lax.rem(t + d, TM)).start()

    filter_frames(False)

    for step in range(PIECES):
        piece = lax.rem(t // 2 + 1 + step, PIECES)
        part = jnp.dot(lhs[...], table[piece], preferred_element_type=F32).astype(BF16)
        for b in range(2):
            to = 2 * piece + b
            own_out[to] = part[:, b * 128 : (b + 1) * 128]

            @pl.when(to != t)
            def _():
                own_copy(to).start()

    own_in[t] = own_out[t]

    @pl.when(t == 0)
    def _():
        ref_halo[1] = jnp.zeros((LOCAL, 128), BF16)

    own_ref = ref_tile(FRAMES, ref_table)

    @pl.when(t > 0)
    def _():
        bytes_of(ref_halo.at[1], ref_sem.at[1])

    ref_out[...] = (own_ref + ref_halo[1].astype(F32)).astype(BF16)
    ref_near[core * 4 + y] = ref_out[...]

    @pl.loop(1, 8)
    def _(d):
        near_copy(d).start()

    def gather_far():
        bytes_of(ref_near.at[pl.ds(0, 7)], ref_sem.at[3])
        for c in range(2):
            packed = jnp.zeros((LOCAL, 128), F32)
            for group in range(4):
                packed = packed + jnp.where(
                    lane // 32 == group, ref_near[c * 4 + group].astype(F32), 0.0
                )
            ref_pack[c * LOCAL : (c + 1) * LOCAL, :] = packed.astype(BF16)
        ref_in[pl.ds(pl.multiple_of(z * 2 * LOCAL, 2 * LOCAL), 2 * LOCAL), :] = ref_pack[...]

        @pl.loop(1, 4)
        def _(d):
            far_copy(d).start()

    def turn(step):
        m = lax.rem(t // 2 + step, TILES)
        blocks = []
        for b in range(2):
            block = 2 * m + b

            @pl.when(block != t)
            def _():
                bytes_of(own_in.at[block], own_rs.at[block])

            @pl.when((block != 0) & (block != t + 1))
            def _():
                bytes_of(spill_in.at[block], spill_rs.at[block])

            own = own_in[block].astype(F32)
            head = own[0:SPILL_ROWS] + spill_in[block].astype(F32)
            own = jnp.concatenate([head, own[SPILL_ROWS:]], axis=0).astype(BF16).astype(F32)
            blocks += [own[f * LOCAL : (f + 1) * LOCAL] for f in range(FRAMES)]
        for to, block in enumerate(butterfly(blocks, lane)):
            send1[m, to * LOCAL : (to + 1) * LOCAL, :] = block.astype(BF16)
        mine = pl.ds(pl.multiple_of(s * LOCAL, LOCAL), LOCAL)
        v[m, mine, :] = send1[m, mine, :]

        @pl.loop(1, STN)
        def _(d):
            turn_copy(m, lax.rem(s + d, STN)).start()

    def send_columns():
        bytes_of(ref_in.at[pl.ds(0, 6 * LOCAL)], ref_sem.at[5])
        row16 = lax.broadcasted_iota(jnp.int32, (2 * K, 1), 0)
        wanted = jnp.zeros((2 * K, 1), jnp.int32)
        for k in range(K):
            wanted = jnp.where(lax.rem(row16, K) == k, basis_in[k], wanted)
        column = lax.broadcasted_iota(jnp.int32, (2 * K, 128), 1)
        onehot = jnp.where(column == lax.rem(wanted, 128), 1.0, 0.0).astype(BF16)
        block = ref_in[...]
        picked = jnp.dot(onehot, block, preferred_element_type=F32)
        picked = jnp.where(lane // 32 == wanted // 128, picked, 0.0)
        picked = picked + pltpu.roll(picked, 64, 1)
        picked = picked + pltpu.roll(picked, 32, 1)
        swapped = jnp.where((lane & 1) == 0, -pltpu.roll(picked, 127, 1), pltpu.roll(picked, 1, 1))
        left = jnp.where(row16 < K, picked, swapped)
        parts = []
        for group in range(4):
            own = jnp.where(lane // 32 == group, left, 0.0).astype(BF16)
            parts.append(
                lax.dot_general(own, block, (((1,), (1,)), ((), ())), preferred_element_type=F32)
            )
        columns = jnp.concatenate(parts, axis=1).astype(BF16)
        cols_out[...] = columns
        cols_in[t] = columns

        @pl.loop(1, TM)
        def _(d):
            columns_copy(lax.rem(t + d, TM)).start()

    def find_basis():
        bytes_of(cols_in.at[pl.ds(0, TM - 1)], cols_sem.at[1])
        columns = cols_in[0].astype(F32)
        for other in range(1, TM):
            columns = columns + cols_in[other].astype(F32)
        columns = columns * (1.0 / SPECTRA)
        basis_re, basis_im = gram_schmidt(columns[0:K], columns[K:])
        basis[0:K, :] = basis_re
        basis[K:, :] = basis_im

    gather_far()
    for step in range(TILES):
        turn(step)
        if step == COLUMNS_AT:
            send_columns()
    find_basis()

    low = basis[...].astype(BF16)
    rows16 = lax.broadcasted_iota(jnp.int32, (16, 128), 0)
    lanes16 = lax.broadcasted_iota(jnp.int32, (16, 128), 1)
    keep = (lanes16 // 64 == rows16 // 8) & (lax.rem(lanes16, 4) == 2 * lax.rem(rows16, 8))
    spectrum = jnp.where(
        lax.rem(lax.broadcasted_iota(jnp.int32, (128, 128), 0) // 4, FRAMES)
        == lax.broadcasted_iota(jnp.int32, (128, 128), 1),
        1.0,
        0.0,
    )
    for step in range(TILES):
        m = lax.rem(t // 2 + step, TILES)
        bytes_of(v.at[m, pl.ds(0, INPUTS - LOCAL)], rs1.at[m])
        z = jnp.dot(low, v[m], preferred_element_type=F32)
        z_re = z[0:K] + pltpu.roll(z[K:], 127, 1)
        z_im = pltpu.roll(z[0:K], 127, 1) - z[K:]
        squares = jnp.sum(z_re * z_re + z_im * z_im, axis=0, keepdims=True)
        both = jnp.dot(
            jnp.where(keep, squares, 0.0), spectrum, precision=HIGHEST, preferred_element_type=F32
        )
        pow_out[2 * m] = both[0:8]
        pow_out[2 * m + 1] = both[8:16]
    pow_in[t] = pow_out[t]

    @pl.loop(1, TM)
    def _(d):
        power_copy(lax.rem(t + d, TM)).start()

    covariances(v, basis, cov, proj, lambda ch: None)

    bytes_of(pow_in.at[pl.ds(0, TM - 1)], pow_rs)
    for owner in range(TM):
        power[2 * owner : 2 * owner + 2, :] = pow_in[owner, 0:2, 0:FRAMES]

    bytes_of(cols_in.at[pl.ds(0, TM - 1)], cols_sem.at[0])
    bytes_of(ref_near.at[pl.ds(0, 7)], ref_sem.at[2])
    bytes_of(ref_in.at[pl.ds(0, 6 * LOCAL)], ref_sem.at[4])

    bytes_of(pow_out.at[pl.ds(0, TM - 1)], pow_ss)
    bytes_of(own_out.at[pl.ds(0, TM - 1)], own_ss)

    @pl.loop(0, TILES)
    def _(m):
        bytes_of(send1.at[m, pl.ds(0, INPUTS - LOCAL)], ss1.at[m])

    @pl.when(t < TM - 1)
    def _():
        bytes_of(ref_halo.at[0], ref_sem.at[0])
        bytes_of(spill_out.at[pl.ds(0, TM - 1)], spill_ss)


def channelise(volt, taps, table, ref_chan, basis_in):
    vmem = pl.BlockSpec(memory_space=pltpu.VMEM)
    hbm = pl.BlockSpec(memory_space=pltpu.HBM)
    dma = pltpu.SemaphoreType.DMA
    return pl.pallas_call(
        channelise_kernel,
        out_shape=(
            pltpu.VMEM((2, INPUTS, 2 * INPUTS), BF16),
            pltpu.VMEM((2, 2 * K * K), F32),
            pltpu.VMEM((16, FRAMES), F32),
        ),
        in_specs=[hbm] * 5,
        out_specs=(vmem, vmem, vmem),
        scratch_shapes=[
            pltpu.VMEM((VOLT_ROWS, 128), jnp.int32),
            pltpu.VMEM((TAPS, NFFT), F32),
            pltpu.SMEM((1,), jnp.int32),
            pltpu.SMEM((K,), jnp.int32),
            pltpu.VMEM((PIECES, 2 * NFFT, 256), BF16),
            pltpu.VMEM((TAPS * Q, 128), F32),
            pltpu.VMEM((FRAMES * LOCAL * Q, 128), F32),
            pltpu.VMEM((FRAMES * LOCAL, 2 * NFFT), BF16),
            pltpu.VMEM((TM, SPILL_ROWS, 128), BF16),
            pltpu.VMEM((TM, SPILL_ROWS, 128), BF16),
            pltpu.VMEM((TM, OWN_ROWS, 128), BF16),
            pltpu.VMEM((TM, OWN_ROWS, 128), BF16),
            pltpu.VMEM((TILES, INPUTS, 128), BF16),
            pltpu.VMEM((2 * K, INPUTS), F32),
            pltpu.VMEM((TILES, INPUTS, 128), BF16),
            pltpu.VMEM((2, LOCAL, 128), BF16),
            pltpu.VMEM((LOCAL, 128), BF16),
            pltpu.VMEM((8, LOCAL, 128), BF16),
            pltpu.VMEM((2 * LOCAL, 128), BF16),
            pltpu.VMEM((8 * LOCAL, 128), BF16),
            pltpu.VMEM((2 * K, INPUTS), BF16),
            pltpu.VMEM((TM, 2 * K, INPUTS), BF16),
            pltpu.VMEM((TM, 8, 128), F32),
            pltpu.VMEM((TM, 8, 128), F32),
            dma((PARTS,)),
            dma((3,)),
            dma,
            dma,
            dma((TM,)),
            dma,
            dma((TM,)),
            dma((TILES,)),
            dma((TILES,)),
            dma((6,)),
            dma((2,)),
            dma,
            dma,
        ],
        compiler_params=pltpu.CompilerParams(
            collective_id=0, has_side_effects=True, vmem_limit_bytes=LIMIT * 1024 * 1024
        ),
        name="channelise",
    )(volt, taps, table, ref_chan, basis_in)


def write_kernel(cov_in, proj_in, power_in, cov, proj, power, sem):
    def store(p):
        rows = pl.ds(p % 2 * (INPUTS // 2), INPUTS // 2)
        return pltpu.make_async_copy(cov_in.at[p // 2, rows], cov.at[p // 2, rows], sem.at[p])

    for p in range(4):
        store(p).start()
    proj[...] = proj_in[...]
    power[...] = power_in[...]
    for p in range(4):
        store(p).wait()


def write(cov, proj, power):
    vmem = pl.BlockSpec(memory_space=pltpu.VMEM)
    hbm = pl.BlockSpec(memory_space=pltpu.HBM)
    return pl.pallas_call(
        write_kernel,
        out_shape=tuple(jax.ShapeDtypeStruct(a.shape, a.dtype) for a in (cov, proj, power)),
        in_specs=[vmem, vmem, vmem],
        out_specs=(hbm, vmem, vmem),
        scratch_shapes=[pltpu.SemaphoreType.DMA((4,))],
        compiler_params=pltpu.CompilerParams(vmem_limit_bytes=16 * 1024 * 1024),
        name="write",
    )(cov, proj, power)


def on_device(table, voltages, filter_taps, reference_channel, basis_inputs):
    volt = voltages.reshape(LOCAL, 2, FRAMES * SUB, 128).transpose(0, 2, 1, 3).reshape(-1, 128)
    volt = pltpu.with_memory_space_constraint(volt, pltpu.HBM)
    table = pltpu.with_memory_space_constraint(table, pltpu.HBM)
    results = channelise(volt, filter_taps, table, reference_channel, basis_inputs)
    return write(*results)


def solution(mesh):
    table = transform_table()

    def whole(voltages, filter_taps, reference_channel, basis_inputs):
        return jax.shard_map(
            on_device,
            mesh=mesh,
            in_specs=(P(), P("stn", None, "tm"), P(), P(), P()),
            out_specs=(P(("stn", "tm"), None, None), P(("stn", "tm"), None), P("stn", "tm")),
            check_vma=False,
        )(jnp.asarray(table), voltages, filter_taps, reference_channel, basis_inputs)

    return whole
```

```python
import functools
import math

import jax
import jax.numpy as jnp
import numpy as np
from jax import lax
from jax.experimental import pallas as pl
from jax.experimental.pallas import tpu as pltpu
from jax.sharding import PartitionSpec as P

NFFT = 1024
FCH = 512
TAPS = 16
K = 8
INPUTS = 512
SPECTRA = 128
STN = 32
TM = 8
LOCAL = INPUTS // STN
FRAMES = SPECTRA // TM
SUB = NFFT // 128
Q = 2 * SUB
SPILL = TAPS - 1
VOLT_ROWS = LOCAL * FRAMES * Q
COLUMNS_AT = 1
PARTS = 4
PIECES = 4
TILES = TM // 2
OWN_ROWS, SPILL_ROWS = FRAMES * LOCAL, SPILL * LOCAL
LIMIT = 56
MESH = pl.DeviceIdType.MESH
F32 = jnp.float32
BF16 = jnp.bfloat16
HIGHEST = lax.Precision.HIGHEST


def transform_table():
    phase = np.arange(NFFT)[:, None] * np.arange(FCH)[None, :] % NFFT
    angle = phase.astype(np.float32) * np.float32(2.0 * math.pi / NFFT)
    factor = np.float32(1.0 / math.sqrt(NFFT))
    cosine, sine = np.cos(angle) * factor, np.sin(angle) * factor
    table_re = np.stack([cosine, -sine], axis=2)
    table_im = np.stack([sine, cosine], axis=2)
    both = np.stack([table_re.reshape(SUB, 128, FCH, 2), table_im.reshape(SUB, 128, FCH, 2)], axis=1)
    both = both.reshape(2 * NFFT, STN, PIECES, 2, 2, 2)
    both = both.transpose(2, 0, 3, 1, 4, 5)
    return both.reshape(PIECES, 2 * NFFT, 256).astype(jnp.bfloat16)


def butterfly(blocks, lane):
    blocks = list(blocks)
    for bit in range(5):
        step, shift = 1 << bit, 4 << bit
        low = (lane & shift) == 0
        for a in range(32):
            if a & step:
                continue
            first, second = blocks[a], blocks[a | step]
            blocks[a] = jnp.where(low, first, pltpu.roll(second, shift, 1))
            blocks[a | step] = jnp.where(low, pltpu.roll(first, 128 - shift, 1), second)
    return blocks


def gram_schmidt(vec_re, vec_im):
    row = lax.broadcasted_iota(jnp.int32, (K, 1), 0)
    for k in range(K):
        w_re, w_im = vec_re[k : k + 1], vec_im[k : k + 1]
        in_re = jnp.sum(w_re * vec_re + w_im * vec_im, axis=1, keepdims=True)
        in_im = jnp.sum(w_re * vec_im - w_im * vec_re, axis=1, keepdims=True)
        inverse = lax.rsqrt(in_re[k : k + 1] + 1e-06)
        q_re, q_im = w_re * inverse, w_im * inverse
        c_re = jnp.where(row > k, in_re * inverse, 0.0)
        c_im = jnp.where(row > k, in_im * inverse, 0.0)
        new_re = vec_re - (q_re * c_re - q_im * c_im)
        new_im = vec_im - (q_re * c_im + q_im * c_re)
        vec_re = jnp.where(row == k, q_re, new_re)
        vec_im = jnp.where(row == k, q_im, new_im)
    return vec_re, vec_im


def covariances(v, basis, cov, proj, done):
    lane4 = lax.broadcasted_iota(jnp.int32, (1, 512), 1)
    x = jnp.concatenate([v[m].astype(F32) for m in range(TILES)], axis=1)
    real = (lane4 & 1) == 0
    swapped = jnp.where(real, pltpu.roll(x, 511, 1), -pltpu.roll(x, 1, 1))
    x_low, swapped = x.astype(BF16), swapped.astype(BF16)
    for ch in range(2):
        keep = (lane4 & 2) == 2 * ch
        for part, left in enumerate((x_low, swapped)):
            left = jnp.where(keep, left, jnp.zeros_like(left))
            prod = lax.dot_general(
                left, x_low, (((1,), (1,)), ((), ())), preferred_element_type=F32
            )
            cov[ch, :, part * INPUTS : (part + 1) * INPUTS] = (prod * (1.0 / SPECTRA)).astype(BF16)
        done(ch)

    b = basis[...]
    b0 = b.astype(BF16)
    rest = b - b0.astype(F32)
    b1 = rest.astype(BF16)
    b2 = (rest - b1.astype(F32)).astype(BF16)
    y = sum(jnp.dot(part, x_low, preferred_element_type=F32) for part in (b2, b1, b0))
    y_re = y[0:K] + pltpu.roll(y[K:], 511, 1)
    y_im = pltpu.roll(y[0:K], 511, 1) - y[K:]
    y = jnp.concatenate([y_re, y_im], axis=0)
    row = lax.broadcasted_iota(jnp.int32, (K, 128), 0)
    col = lax.broadcasted_iota(jnp.int32, (K, 128), 1)
    for ch in range(2):
        left = jnp.where((lane4 & 3) == 2 * ch, y, 0.0)
        gram = lax.dot_general(
            left, y, (((1,), (1,)), ((), ())), precision=HIGHEST, preferred_element_type=F32
        )
        re = gram[0:K, 0:K] + gram[K:, K:]
        im = gram[K:, 0:K] - gram[0:K, K:]
        flat = jnp.concatenate([re] * K + [im] * K, axis=1)
        flat = jnp.where(lax.rem(col // K, K) == row, flat, 0.0)
        proj[ch : ch + 1, :] = jnp.sum(flat, axis=0, keepdims=True) * (1.0 / SPECTRA)


def channelise_kernel(
    volt_hbm, taps_hbm, table_hbm, ref_hbm, basis_hbm,
    cov, proj, power,
    volt, taps, ref_chan, basis_in, table, tap_rows, frames_f, lhs, spill_out, spill_in, own_out, own_in,
    v, basis, send1, ref_halo, ref_out, ref_near, ref_pack, ref_in, cols_out, cols_in, pow_out, pow_in,
    volt_sem, small_sem, table_sem, spill_ss, spill_rs, own_ss, own_rs, ss1, rs1, ref_sem, cols_sem, pow_ss, pow_rs,
):
    s = lax.axis_index("stn")
    t = lax.axis_index("tm")
    load_taps = pltpu.make_async_copy(taps_hbm, taps, small_sem.at[0])
    load_taps.start()
    load_ref = pltpu.make_async_copy(ref_hbm, ref_chan, small_sem.at[1])
    load_ref.start()
    load_basis = pltpu.make_async_copy(basis_hbm, basis_in, small_sem.at[2])
    load_basis.start()

    def load_volt(part):
        rows = pl.ds(pl.multiple_of(part * (VOLT_ROWS // PARTS), 8), VOLT_ROWS // PARTS)
        return pltpu.make_async_copy(volt_hbm.at[rows], volt.at[rows], volt_sem.at[part])

    for part in range(PARTS):
        load_volt(part).start()
    load_table = pltpu.make_async_copy(table_hbm, table, table_sem)
    load_table.start()

    barrier = pltpu.get_barrier_semaphore()

    @pl.loop(1, STN)
    def _(d):
        pl.semaphore_signal(barrier, 1, device_id={"stn": lax.rem(s + d, STN)}, device_id_type=MESH)

    @pl.loop(1, TM)
    def _(d):
        pl.semaphore_signal(barrier, 1, device_id={"tm": lax.rem(t + d, TM)}, device_id_type=MESH)

    load_taps.wait()
    for sub in range(SUB):
        part = taps[:, sub * 128 : (sub + 1) * 128] * (1.0 / 64.0)
        for p in range(2):
            tap_rows[pl.ds(sub * 2 + p, TAPS, stride=Q), :] = part

    def filter_frames(spill):
        @pl.loop(0, LOCAL * 2)
        def _(step):
            if spill:
                @pl.when(lax.rem(step, LOCAL * 2 // PARTS) == 0)
                def _():
                    load_volt(step // (LOCAL * 2 // PARTS)).wait()

            i, half = step // 2, lax.rem(step, 2)
            base = pl.multiple_of(i * (FRAMES * Q) + half * 8, 8)
            x = [volt[pl.ds(base + f * Q, 8), :].astype(F32) for f in range(FRAMES)]
            tap = [tap_rows[pl.ds(pl.multiple_of(k * Q + half * 8, 8), 8), :] for k in range(TAPS)]
            for f in range(SPILL if spill else FRAMES):
                acc = None
                for j in range(f + 1, FRAMES) if spill else range(f + 1):
                    k = j - f - 1 if spill else SPILL - f + j
                    term = tap[k] * x[j]
                    acc = term if acc is None else acc + term
                row = pl.multiple_of((f * LOCAL + i) * Q + half * 8, 8)
                frames_f[pl.ds(row, 8), :] = acc

        rows = (SPILL if spill else FRAMES) * LOCAL
        for q in range(Q):
            lhs[0:rows, q * 128 : (q + 1) * 128] = frames_f[pl.ds(q, rows, stride=Q), :].astype(BF16)

    def spill_copy(to):
        return pltpu.make_async_remote_copy(
            src_ref=spill_out.at[to],
            dst_ref=spill_in.at[lax.rem(t + 1, TM)],
            send_sem=spill_ss,
            recv_sem=spill_rs.at[lax.rem(t + 1, TM)],
            device_id={"tm": to},
            device_id_type=MESH,
        )

    def own_copy(to):
        return pltpu.make_async_remote_copy(
            src_ref=own_out.at[to],
            dst_ref=own_in.at[t],
            send_sem=own_ss,
            recv_sem=own_rs.at[t],
            device_id={"tm": to},
            device_id_type=MESH,
        )

    def turn_copy(m, to):
        return pltpu.make_async_remote_copy(
            src_ref=send1.at[m, pl.ds(pl.multiple_of(to * LOCAL, LOCAL), LOCAL)],
            dst_ref=v.at[m, pl.ds(pl.multiple_of(s * LOCAL, LOCAL), LOCAL)],
            send_sem=ss1.at[m],
            recv_sem=rs1.at[m],
            device_id={"stn": to},
            device_id_type=MESH,
        )

    def power_copy(to):
        return pltpu.make_async_remote_copy(
            src_ref=pow_out.at[to],
            dst_ref=pow_in.at[t],
            send_sem=pow_ss,
            recv_sem=pow_rs,
            device_id={"tm": to},
            device_id_type=MESH,
        )

    def bytes_of(ref, sem):
        pltpu.make_async_copy(ref, ref, sem).wait()

    lane = lax.broadcasted_iota(jnp.int32, (1, 128), 1)

    def ref_tile(rows, ref_table):
        part = jnp.dot(lhs[0 : rows * LOCAL, :], ref_table, preferred_element_type=F32)
        total = jnp.zeros((LOCAL, 128), F32)
        for f in range(rows):
            total = total + jnp.where(
                lax.rem(lane // 2, FRAMES) == f, part[f * LOCAL : (f + 1) * LOCAL], 0.0
            )
        return total

    def ref_halo_copy():
        return pltpu.make_async_remote_copy(
            src_ref=ref_halo.at[0],
            dst_ref=ref_halo.at[1],
            send_sem=ref_sem.at[0],
            recv_sem=ref_sem.at[1],
            device_id={"tm": lax.rem(t + 1, TM)},
            device_id_type=MESH,
        )

    y, z, core = s // 8, lax.rem(s // 2, 4), lax.rem(s, 2)

    def near_copy(d):
        to = lax.rem(y * 2 + core + d, 8)
        return pltpu.make_async_remote_copy(
            src_ref=ref_out,
            dst_ref=ref_near.at[core * 4 + y],
            send_sem=ref_sem.at[2],
            recv_sem=ref_sem.at[3],
            device_id={"stn": to // 2 * 8 + z * 2 + lax.rem(to, 2)},
            device_id_type=MESH,
        )

    def far_copy(d):
        return pltpu.make_async_remote_copy(
            src_ref=ref_pack,
            dst_ref=ref_in.at[pl.ds(pl.multiple_of(z * 2 * LOCAL, 2 * LOCAL), 2 * LOCAL)],
            send_sem=ref_sem.at[4],
            recv_sem=ref_sem.at[5],
            device_id={"stn": y * 8 + lax.rem(z + d, 4) * 2 + core},
            device_id_type=MESH,
        )

    def columns_copy(to):
        return pltpu.make_async_remote_copy(
            src_ref=cols_out,
            dst_ref=cols_in.at[t],
            send_sem=cols_sem.at[0],
            recv_sem=cols_sem.at[1],
            device_id={"tm": to},
            device_id_type=MESH,
        )

    filter_frames(True)
    load_table.wait()
    load_ref.wait()
    load_basis.wait()
    ref = ref_chan[0]
    ref_stn, ref_tm, ref_low = ref // 16, lax.rem(ref // 2, TM), lax.rem(ref, 2)
    ref_at = lax.rem(ref_tm, 2) * 128 + ref_stn * 4 + ref_low * 2
    chosen = lax.broadcasted_iota(jnp.int32, (256, 128), 0) == ref_at + (lane & 1)
    ref_table = jnp.dot(
        table[ref_tm // 2],
        jnp.where(chosen, 1.0, 0.0).astype(BF16),
        preferred_element_type=F32,
    ).astype(BF16)
    ref_halo[0] = ref_tile(SPILL, ref_table).astype(BF16)
    spill_in[0] = jnp.zeros((SPILL_ROWS, 128), BF16)
    pl.semaphore_wait(barrier, STN - 1 + TM - 1)

    @pl.when(t < TM - 1)
    def _():
        ref_halo_copy().start()

    for step in range(PIECES):
        piece = lax.rem(t // 2 + 1 + step, PIECES)
        part = jnp.dot(lhs[0:SPILL_ROWS, :], table[piece], preferred_element_type=F32).astype(BF16)
        for b in range(2):
            to = 2 * piece + b
            spill_out[to] = part[:, b * 128 : (b + 1) * 128]

            @pl.when((t < TM - 1) & (to != t))
            def _():
                spill_copy(to).start()

    @pl.when(t < TM - 1)
    def _():
        spill_in[t + 1] = spill_out[t]

    filter_frames(False)

    for step in range(PIECES):
        piece = lax.rem(t // 2 + 1 + step, PIECES)
        part = jnp.dot(lhs[...], table[piece], preferred_element_type=F32).astype(BF16)
        for b in range(2):
            to = 2 * piece + b
            own_out[to] = part[:, b * 128 : (b + 1) * 128]

            @pl.when(to != t)
            def _():
                own_copy(to).start()

    own_in[t] = own_out[t]

    @pl.when(t == 0)
    def _():
        ref_halo[1] = jnp.zeros((LOCAL, 128), BF16)

    own_ref = ref_tile(FRAMES, ref_table)

    @pl.when(t > 0)
    def _():
        bytes_of(ref_halo.at[1], ref_sem.at[1])

    ref_out[...] = (own_ref + ref_halo[1].astype(F32)).astype(BF16)
    ref_near[core * 4 + y] = ref_out[...]

    @pl.loop(1, 8)
    def _(d):
        near_copy(d).start()

    def gather_far():
        bytes_of(ref_near.at[pl.ds(0, 7)], ref_sem.at[3])
        for c in range(2):
            packed = jnp.zeros((LOCAL, 128), F32)
            for group in range(4):
                packed = packed + jnp.where(
                    lane // 32 == group, ref_near[c * 4 + group].astype(F32), 0.0
                )
            ref_pack[c * LOCAL : (c + 1) * LOCAL, :] = packed.astype(BF16)
        ref_in[pl.ds(pl.multiple_of(z * 2 * LOCAL, 2 * LOCAL), 2 * LOCAL), :] = ref_pack[...]

        @pl.loop(1, 4)
        def _(d):
            far_copy(d).start()

    def turn(step):
        m = lax.rem(t // 2 + TILES - 1 - step, TILES)
        blocks = []
        for b in range(2):
            block = 2 * m + b

            @pl.when(block != t)
            def _():
                bytes_of(own_in.at[block], own_rs.at[block])

            @pl.when((block != 0) & (block != t + 1))
            def _():
                bytes_of(spill_in.at[block], spill_rs.at[block])

            own = own_in[block].astype(F32)
            head = own[0:SPILL_ROWS] + spill_in[block].astype(F32)
            own = jnp.concatenate([head, own[SPILL_ROWS:]], axis=0).astype(BF16).astype(F32)
            blocks += [own[f * LOCAL : (f + 1) * LOCAL] for f in range(FRAMES)]
        for to, block in enumerate(butterfly(blocks, lane)):
            send1[m, to * LOCAL : (to + 1) * LOCAL, :] = block.astype(BF16)
        mine = pl.ds(pl.multiple_of(s * LOCAL, LOCAL), LOCAL)
        v[m, mine, :] = send1[m, mine, :]

        for away in (2, 1, 3, 0):
            @pl.loop(0 if away else 1, 8)
            def _(d):
                near = lax.rem(y * 2 + core + d, 8)
                to = near // 2 * 8 + lax.rem(z + away, 4) * 2 + lax.rem(near, 2)
                turn_copy(m, to).start()

    def send_columns():
        bytes_of(ref_in.at[pl.ds(0, 6 * LOCAL)], ref_sem.at[5])
        row16 = lax.broadcasted_iota(jnp.int32, (2 * K, 1), 0)
        wanted = jnp.zeros((2 * K, 1), jnp.int32)
        for k in range(K):
            wanted = jnp.where(lax.rem(row16, K) == k, basis_in[k], wanted)
        column = lax.broadcasted_iota(jnp.int32, (2 * K, 128), 1)
        onehot = jnp.where(column == lax.rem(wanted, 128), 1.0, 0.0).astype(BF16)
        block = ref_in[...]
        picked = jnp.dot(onehot, block, preferred_element_type=F32)
        picked = jnp.where(lane // 32 == wanted // 128, picked, 0.0)
        picked = picked + pltpu.roll(picked, 64, 1)
        picked = picked + pltpu.roll(picked, 32, 1)
        swapped = jnp.where((lane & 1) == 0, -pltpu.roll(picked, 127, 1), pltpu.roll(picked, 1, 1))
        left = jnp.where(row16 < K, picked, swapped)
        parts = []
        for group in range(4):
            own = jnp.where(lane // 32 == group, left, 0.0).astype(BF16)
            parts.append(
                lax.dot_general(own, block, (((1,), (1,)), ((), ())), preferred_element_type=F32)
            )
        columns = jnp.concatenate(parts, axis=1).astype(BF16)
        cols_out[...] = columns
        cols_in[t] = columns

        @pl.loop(1, TM)
        def _(d):
            columns_copy(lax.rem(t + d, TM)).start()

    def find_basis():
        bytes_of(cols_in.at[pl.ds(0, TM - 1)], cols_sem.at[1])
        columns = cols_in[0].astype(F32)
        for other in range(1, TM):
            columns = columns + cols_in[other].astype(F32)
        columns = columns * (1.0 / SPECTRA)
        basis_re, basis_im = gram_schmidt(columns[0:K], columns[K:])
        basis[0:K, :] = basis_re
        basis[K:, :] = basis_im

    gather_far()
    for step in range(TILES):
        turn(step)
        if step == COLUMNS_AT:
            send_columns()
    find_basis()

    low = basis[...].astype(BF16)
    rows16 = lax.broadcasted_iota(jnp.int32, (16, 128), 0)
    lanes16 = lax.broadcasted_iota(jnp.int32, (16, 128), 1)
    keep = (lanes16 // 64 == rows16 // 8) & (lax.rem(lanes16, 4) == 2 * lax.rem(rows16, 8))
    spectrum = jnp.where(
        lax.rem(lax.broadcasted_iota(jnp.int32, (128, 128), 0) // 4, FRAMES)
        == lax.broadcasted_iota(jnp.int32, (128, 128), 1),
        1.0,
        0.0,
    )
    for step in range(TILES):
        m = lax.rem(t // 2 + TILES - 1 - step, TILES)
        bytes_of(v.at[m, pl.ds(0, INPUTS - LOCAL)], rs1.at[m])
        z = jnp.dot(low, v[m], preferred_element_type=F32)
        z_re = z[0:K] + pltpu.roll(z[K:], 127, 1)
        z_im = pltpu.roll(z[0:K], 127, 1) - z[K:]
        squares = jnp.sum(z_re * z_re + z_im * z_im, axis=0, keepdims=True)
        both = jnp.dot(
            jnp.where(keep, squares, 0.0), spectrum, precision=HIGHEST, preferred_element_type=F32
        )
        pow_out[2 * m] = both[0:8]
        pow_out[2 * m + 1] = both[8:16]
    pow_in[t] = pow_out[t]

    @pl.loop(1, TM)
    def _(d):
        power_copy(lax.rem(t + d, TM)).start()

    covariances(v, basis, cov, proj, lambda ch: None)

    bytes_of(pow_in.at[pl.ds(0, TM - 1)], pow_rs)
    for owner in range(TM):
        power[2 * owner : 2 * owner + 2, :] = pow_in[owner, 0:2, 0:FRAMES]

    bytes_of(cols_in.at[pl.ds(0, TM - 1)], cols_sem.at[0])
    bytes_of(ref_near.at[pl.ds(0, 7)], ref_sem.at[2])
    bytes_of(ref_in.at[pl.ds(0, 6 * LOCAL)], ref_sem.at[4])

    bytes_of(pow_out.at[pl.ds(0, TM - 1)], pow_ss)
    bytes_of(own_out.at[pl.ds(0, TM - 1)], own_ss)

    @pl.loop(0, TILES)
    def _(m):
        bytes_of(send1.at[m, pl.ds(0, INPUTS - LOCAL)], ss1.at[m])

    @pl.when(t < TM - 1)
    def _():
        bytes_of(ref_halo.at[0], ref_sem.at[0])
        bytes_of(spill_out.at[pl.ds(0, TM - 1)], spill_ss)


def channelise(volt, taps, table, ref_chan, basis_in):
    vmem = pl.BlockSpec(memory_space=pltpu.VMEM)
    hbm = pl.BlockSpec(memory_space=pltpu.HBM)
    dma = pltpu.SemaphoreType.DMA
    return pl.pallas_call(
        channelise_kernel,
        out_shape=(
            pltpu.VMEM((2, INPUTS, 2 * INPUTS), BF16),
            pltpu.VMEM((2, 2 * K * K), F32),
            pltpu.VMEM((16, FRAMES), F32),
        ),
        in_specs=[hbm] * 5,
        out_specs=(vmem, vmem, vmem),
        scratch_shapes=[
            pltpu.VMEM((VOLT_ROWS, 128), jnp.int32),
            pltpu.VMEM((TAPS, NFFT), F32),
            pltpu.SMEM((1,), jnp.int32),
            pltpu.SMEM((K,), jnp.int32),
            pltpu.VMEM((PIECES, 2 * NFFT, 256), BF16),
            pltpu.VMEM((TAPS * Q, 128), F32),
            pltpu.VMEM((FRAMES * LOCAL * Q, 128), F32),
            pltpu.VMEM((FRAMES * LOCAL, 2 * NFFT), BF16),
            pltpu.VMEM((TM, SPILL_ROWS, 128), BF16),
            pltpu.VMEM((TM, SPILL_ROWS, 128), BF16),
            pltpu.VMEM((TM, OWN_ROWS, 128), BF16),
            pltpu.VMEM((TM, OWN_ROWS, 128), BF16),
            pltpu.VMEM((TILES, INPUTS, 128), BF16),
            pltpu.VMEM((2 * K, INPUTS), F32),
            pltpu.VMEM((TILES, INPUTS, 128), BF16),
            pltpu.VMEM((2, LOCAL, 128), BF16),
            pltpu.VMEM((LOCAL, 128), BF16),
            pltpu.VMEM((8, LOCAL, 128), BF16),
            pltpu.VMEM((2 * LOCAL, 128), BF16),
            pltpu.VMEM((8 * LOCAL, 128), BF16),
            pltpu.VMEM((2 * K, INPUTS), BF16),
            pltpu.VMEM((TM, 2 * K, INPUTS), BF16),
            pltpu.VMEM((TM, 8, 128), F32),
            pltpu.VMEM((TM, 8, 128), F32),
            dma((PARTS,)),
            dma((3,)),
            dma,
            dma,
            dma((TM,)),
            dma,
            dma((TM,)),
            dma((TILES,)),
            dma((TILES,)),
            dma((6,)),
            dma((2,)),
            dma,
            dma,
        ],
        compiler_params=pltpu.CompilerParams(
            collective_id=0, has_side_effects=True, vmem_limit_bytes=LIMIT * 1024 * 1024
        ),
        name="channelise",
    )(volt, taps, table, ref_chan, basis_in)


def write_kernel(cov_in, proj_in, power_in, cov, proj, power, sem):
    def store(p):
        rows = pl.ds(p % 2 * (INPUTS // 2), INPUTS // 2)
        return pltpu.make_async_copy(cov_in.at[p // 2, rows], cov.at[p // 2, rows], sem.at[p])

    for p in range(4):
        store(p).start()
    proj[...] = proj_in[...]
    power[...] = power_in[...]
    for p in range(4):
        store(p).wait()


def write(cov, proj, power):
    vmem = pl.BlockSpec(memory_space=pltpu.VMEM)
    hbm = pl.BlockSpec(memory_space=pltpu.HBM)
    return pl.pallas_call(
        write_kernel,
        out_shape=tuple(jax.ShapeDtypeStruct(a.shape, a.dtype) for a in (cov, proj, power)),
        in_specs=[vmem, vmem, vmem],
        out_specs=(hbm, vmem, vmem),
        scratch_shapes=[pltpu.SemaphoreType.DMA((4,))],
        compiler_params=pltpu.CompilerParams(vmem_limit_bytes=16 * 1024 * 1024),
        name="write",
    )(cov, proj, power)


def on_device(table, voltages, filter_taps, reference_channel, basis_inputs):
    volt = voltages.reshape(LOCAL, 2, FRAMES * SUB, 128).transpose(0, 2, 1, 3).reshape(-1, 128)
    volt = pltpu.with_memory_space_constraint(volt, pltpu.HBM)
    table = pltpu.with_memory_space_constraint(table, pltpu.HBM)
    results = channelise(volt, filter_taps, table, reference_channel, basis_inputs)
    return write(*results)


def solution(mesh):
    table = transform_table()

    def whole(voltages, filter_taps, reference_channel, basis_inputs):
        return jax.shard_map(
            on_device,
            mesh=mesh,
            in_specs=(P(), P("stn", None, "tm"), P(), P(), P()),
            out_specs=(P(("stn", "tm"), None, None), P(("stn", "tm"), None), P("stn", "tm")),
            check_vma=False,
        )(jnp.asarray(table), voltages, filter_taps, reference_channel, basis_inputs)

    return whole
```

```python
import functools
import math

import jax
import jax.numpy as jnp
import numpy as np
from jax import lax
from jax.experimental import pallas as pl
from jax.experimental.pallas import tpu as pltpu
from jax.sharding import PartitionSpec as P

NFFT = 1024
FCH = 512
TAPS = 16
K = 8
INPUTS = 512
SPECTRA = 128
STN = 32
TM = 8
LOCAL = INPUTS // STN
FRAMES = SPECTRA // TM
SUB = NFFT // 128
Q = 2 * SUB
SPILL = TAPS - 1
VOLT_ROWS = LOCAL * FRAMES * Q
COLUMNS_AT = 1
PARTS = 4
PIECES = 4
TILES = TM // 2
OWN_ROWS, SPILL_ROWS = FRAMES * LOCAL, SPILL * LOCAL
LIMIT = 56
MESH = pl.DeviceIdType.MESH
F32 = jnp.float32
BF16 = jnp.bfloat16
HIGHEST = lax.Precision.HIGHEST


def transform_table():
    phase = np.arange(NFFT)[:, None] * np.arange(FCH)[None, :] % NFFT
    angle = phase.astype(np.float32) * np.float32(2.0 * math.pi / NFFT)
    factor = np.float32(1.0 / math.sqrt(NFFT))
    cosine, sine = np.cos(angle) * factor, np.sin(angle) * factor
    table_re = np.stack([cosine, -sine], axis=2)
    table_im = np.stack([sine, cosine], axis=2)
    both = np.stack([table_re.reshape(SUB, 128, FCH, 2), table_im.reshape(SUB, 128, FCH, 2)], axis=1)
    both = both.reshape(2 * NFFT, STN, PIECES, 2, 2, 2)
    both = both.transpose(2, 0, 3, 1, 4, 5)
    return both.reshape(PIECES, 2 * NFFT, 256).astype(jnp.bfloat16)


def butterfly(blocks, lane):
    blocks = list(blocks)
    for bit in range(5):
        step, shift = 1 << bit, 4 << bit
        low = (lane & shift) == 0
        for a in range(32):
            if a & step:
                continue
            first, second = blocks[a], blocks[a | step]
            blocks[a] = jnp.where(low, first, pltpu.roll(second, shift, 1))
            blocks[a | step] = jnp.where(low, pltpu.roll(first, 128 - shift, 1), second)
    return blocks


def gram_schmidt(vec_re, vec_im):
    row = lax.broadcasted_iota(jnp.int32, (K, 1), 0)
    for k in range(K):
        w_re, w_im = vec_re[k : k + 1], vec_im[k : k + 1]
        in_re = jnp.sum(w_re * vec_re + w_im * vec_im, axis=1, keepdims=True)
        in_im = jnp.sum(w_re * vec_im - w_im * vec_re, axis=1, keepdims=True)
        inverse = lax.rsqrt(in_re[k : k + 1] + 1e-06)
        q_re, q_im = w_re * inverse, w_im * inverse
        c_re = jnp.where(row > k, in_re * inverse, 0.0)
        c_im = jnp.where(row > k, in_im * inverse, 0.0)
        new_re = vec_re - (q_re * c_re - q_im * c_im)
        new_im = vec_im - (q_re * c_im + q_im * c_re)
        vec_re = jnp.where(row == k, q_re, new_re)
        vec_im = jnp.where(row == k, q_im, new_im)
    return vec_re, vec_im


def covariances(v, basis, cov, proj, done):
    lane4 = lax.broadcasted_iota(jnp.int32, (1, 512), 1)
    x = jnp.concatenate([v[m].astype(F32) for m in range(TILES)], axis=1)
    real = (lane4 & 1) == 0
    swapped = jnp.where(real, pltpu.roll(x, 511, 1), -pltpu.roll(x, 1, 1))
    x_low, swapped = x.astype(BF16), swapped.astype(BF16)
    for ch in range(2):
        keep = (lane4 & 2) == 2 * ch
        for part, left in enumerate((x_low, swapped)):
            left = jnp.where(keep, left, jnp.zeros_like(left))
            prod = lax.dot_general(
                left, x_low, (((1,), (1,)), ((), ())), preferred_element_type=F32
            )
            cov[ch, :, part * INPUTS : (part + 1) * INPUTS] = (prod * (1.0 / SPECTRA)).astype(BF16)
        done(ch)

    b = basis[...]
    b0 = b.astype(BF16)
    rest = b - b0.astype(F32)
    b1 = rest.astype(BF16)
    b2 = (rest - b1.astype(F32)).astype(BF16)
    y = sum(jnp.dot(part, x_low, preferred_element_type=F32) for part in (b2, b1, b0))
    y_re = y[0:K] + pltpu.roll(y[K:], 511, 1)
    y_im = pltpu.roll(y[0:K], 511, 1) - y[K:]
    y = jnp.concatenate([y_re, y_im], axis=0)
    row = lax.broadcasted_iota(jnp.int32, (K, 128), 0)
    col = lax.broadcasted_iota(jnp.int32, (K, 128), 1)
    for ch in range(2):
        left = jnp.where((lane4 & 3) == 2 * ch, y, 0.0)
        gram = lax.dot_general(
            left, y, (((1,), (1,)), ((), ())), precision=HIGHEST, preferred_element_type=F32
        )
        re = gram[0:K, 0:K] + gram[K:, K:]
        im = gram[K:, 0:K] - gram[0:K, K:]
        flat = jnp.concatenate([re] * K + [im] * K, axis=1)
        flat = jnp.where(lax.rem(col // K, K) == row, flat, 0.0)
        proj[ch : ch + 1, :] = jnp.sum(flat, axis=0, keepdims=True) * (1.0 / SPECTRA)


def channelise_kernel(
    volt_hbm, taps_hbm, table_hbm, ref_hbm, basis_hbm,
    cov, proj, power,
    volt, taps, ref_chan, basis_in, table, tap_rows, frames_f, lhs, spill_out, spill_in, own_out, own_in,
    v, basis, send1, ref_halo, ref_out, ref_near, ref_pack, ref_in, cols_out, cols_in, pow_out, pow_in,
    volt_sem, small_sem, table_sem, spill_ss, spill_rs, own_ss, own_rs, ss1, rs1, ref_sem, cols_sem, pow_ss, pow_rs,
):
    s = lax.axis_index("stn")
    t = lax.axis_index("tm")
    load_taps = pltpu.make_async_copy(taps_hbm, taps, small_sem.at[0])
    load_taps.start()
    load_ref = pltpu.make_async_copy(ref_hbm, ref_chan, small_sem.at[1])
    load_ref.start()
    load_basis = pltpu.make_async_copy(basis_hbm, basis_in, small_sem.at[2])
    load_basis.start()

    def load_volt(part):
        rows = pl.ds(pl.multiple_of(part * (VOLT_ROWS // PARTS), 8), VOLT_ROWS // PARTS)
        return pltpu.make_async_copy(volt_hbm.at[rows], volt.at[rows], volt_sem.at[part])

    for part in range(PARTS):
        load_volt(part).start()
    load_table = pltpu.make_async_copy(table_hbm, table, table_sem)
    load_table.start()

    barrier = pltpu.get_barrier_semaphore()

    for away in (2, 1, 3, 0):
        @pl.loop(0 if away else 1, 8)
        def _(d):
            near = lax.rem(s // 8 * 2 + lax.rem(s, 2) + d, 8)
            to = near // 2 * 8 + lax.rem(s // 2 + away, 4) * 2 + lax.rem(near, 2)
            pl.semaphore_signal(barrier, 1, device_id={"stn": to}, device_id_type=MESH)

    @pl.loop(1, TM)
    def _(d):
        pl.semaphore_signal(barrier, 1, device_id={"tm": lax.rem(t + d, TM)}, device_id_type=MESH)

    load_taps.wait()
    for sub in range(SUB):
        part = taps[:, sub * 128 : (sub + 1) * 128] * (1.0 / 64.0)
        for p in range(2):
            tap_rows[pl.ds(sub * 2 + p, TAPS, stride=Q), :] = part

    def filter_frames(spill):
        @pl.loop(0, LOCAL * 2)
        def _(step):
            if spill:
                @pl.when(lax.rem(step, LOCAL * 2 // PARTS) == 0)
                def _():
                    load_volt(step // (LOCAL * 2 // PARTS)).wait()

            i, half = step // 2, lax.rem(step, 2)
            base = pl.multiple_of(i * (FRAMES * Q) + half * 8, 8)
            x = [volt[pl.ds(base + f * Q, 8), :].astype(F32) for f in range(FRAMES)]
            tap = [tap_rows[pl.ds(pl.multiple_of(k * Q + half * 8, 8), 8), :] for k in range(TAPS)]
            for f in range(SPILL if spill else FRAMES):
                acc = None
                for j in range(f + 1, FRAMES) if spill else range(f + 1):
                    k = j - f - 1 if spill else SPILL - f + j
                    term = tap[k] * x[j]
                    acc = term if acc is None else acc + term
                row = pl.multiple_of((f * LOCAL + i) * Q + half * 8, 8)
                frames_f[pl.ds(row, 8), :] = acc

        rows = (SPILL if spill else FRAMES) * LOCAL
        for q in range(Q):
            lhs[0:rows, q * 128 : (q + 1) * 128] = frames_f[pl.ds(q, rows, stride=Q), :].astype(BF16)

    def spill_copy(to):
        return pltpu.make_async_remote_copy(
            src_ref=spill_out.at[to],
            dst_ref=spill_in.at[lax.rem(t + 1, TM)],
            send_sem=spill_ss,
            recv_sem=spill_rs.at[lax.rem(t + 1, TM)],
            device_id={"tm": to},
            device_id_type=MESH,
        )

    def own_copy(to):
        return pltpu.make_async_remote_copy(
            src_ref=own_out.at[to],
            dst_ref=own_in.at[t],
            send_sem=own_ss,
            recv_sem=own_rs.at[t],
            device_id={"tm": to},
            device_id_type=MESH,
        )

    def turn_copy(m, to):
        return pltpu.make_async_remote_copy(
            src_ref=send1.at[m, pl.ds(pl.multiple_of(to * LOCAL, LOCAL), LOCAL)],
            dst_ref=v.at[m, pl.ds(pl.multiple_of(s * LOCAL, LOCAL), LOCAL)],
            send_sem=ss1.at[m],
            recv_sem=rs1.at[m],
            device_id={"stn": to},
            device_id_type=MESH,
        )

    def power_copy(to):
        return pltpu.make_async_remote_copy(
            src_ref=pow_out.at[to],
            dst_ref=pow_in.at[t],
            send_sem=pow_ss,
            recv_sem=pow_rs,
            device_id={"tm": to},
            device_id_type=MESH,
        )

    def bytes_of(ref, sem):
        pltpu.make_async_copy(ref, ref, sem).wait()

    lane = lax.broadcasted_iota(jnp.int32, (1, 128), 1)

    def ref_tile(rows, ref_table):
        part = jnp.dot(lhs[0 : rows * LOCAL, :], ref_table, preferred_element_type=F32)
        total = jnp.zeros((LOCAL, 128), F32)
        for f in range(rows):
            total = total + jnp.where(
                lax.rem(lane // 2, FRAMES) == f, part[f * LOCAL : (f + 1) * LOCAL], 0.0
            )
        return total

    def ref_halo_copy():
        return pltpu.make_async_remote_copy(
            src_ref=ref_halo.at[0],
            dst_ref=ref_halo.at[1],
            send_sem=ref_sem.at[0],
            recv_sem=ref_sem.at[1],
            device_id={"tm": lax.rem(t + 1, TM)},
            device_id_type=MESH,
        )

    y, z, core = s // 8, lax.rem(s // 2, 4), lax.rem(s, 2)

    def near_copy(d):
        to = lax.rem(y * 2 + core + d, 8)
        return pltpu.make_async_remote_copy(
            src_ref=ref_out,
            dst_ref=ref_near.at[core * 4 + y],
            send_sem=ref_sem.at[2],
            recv_sem=ref_sem.at[3],
            device_id={"stn": to // 2 * 8 + z * 2 + lax.rem(to, 2)},
            device_id_type=MESH,
        )

    def far_copy(d):
        return pltpu.make_async_remote_copy(
            src_ref=ref_pack,
            dst_ref=ref_in.at[pl.ds(pl.multiple_of(z * 2 * LOCAL, 2 * LOCAL), 2 * LOCAL)],
            send_sem=ref_sem.at[4],
            recv_sem=ref_sem.at[5],
            device_id={"stn": y * 8 + lax.rem(z + d, 4) * 2 + core},
            device_id_type=MESH,
        )

    def columns_copy(to):
        return pltpu.make_async_remote_copy(
            src_ref=cols_out,
            dst_ref=cols_in.at[t],
            send_sem=cols_sem.at[0],
            recv_sem=cols_sem.at[1],
            device_id={"tm": to},
            device_id_type=MESH,
        )

    filter_frames(True)
    load_table.wait()
    load_ref.wait()
    load_basis.wait()
    ref = ref_chan[0]
    ref_stn, ref_tm, ref_low = ref // 16, lax.rem(ref // 2, TM), lax.rem(ref, 2)
    ref_at = lax.rem(ref_tm, 2) * 128 + ref_stn * 4 + ref_low * 2
    chosen = lax.broadcasted_iota(jnp.int32, (256, 128), 0) == ref_at + (lane & 1)
    ref_table = jnp.dot(
        table[ref_tm // 2],
        jnp.where(chosen, 1.0, 0.0).astype(BF16),
        preferred_element_type=F32,
    ).astype(BF16)
    ref_halo[0] = ref_tile(SPILL, ref_table).astype(BF16)
    spill_in[0] = jnp.zeros((SPILL_ROWS, 128), BF16)
    pl.semaphore_wait(barrier, STN - 1 + TM - 1)

    @pl.when(t < TM - 1)
    def _():
        ref_halo_copy().start()

    for step in range(PIECES):
        piece = lax.rem(t // 2 + 1 + step, PIECES)
        part = jnp.dot(lhs[0:SPILL_ROWS, :], table[piece], preferred_element_type=F32).astype(BF16)
        for b in range(2):
            to = 2 * piece + b
            spill_out[to] = part[:, b * 128 : (b + 1) * 128]

            @pl.when((t < TM - 1) & (to != t))
            def _():
                spill_copy(to).start()

    @pl.when(t < TM - 1)
    def _():
        spill_in[t + 1] = spill_out[t]

    filter_frames(False)

    for step in range(PIECES):
        piece = lax.rem(t // 2 + 1 + step, PIECES)
        part = jnp.dot(lhs[...], table[piece], preferred_element_type=F32).astype(BF16)
        for b in range(2):
            to = 2 * piece + b
            own_out[to] = part[:, b * 128 : (b + 1) * 128]

            @pl.when(to != t)
            def _():
                own_copy(to).start()

    own_in[t] = own_out[t]

    @pl.when(t == 0)
    def _():
        ref_halo[1] = jnp.zeros((LOCAL, 128), BF16)

    own_ref = ref_tile(FRAMES, ref_table)

    @pl.when(t > 0)
    def _():
        bytes_of(ref_halo.at[1], ref_sem.at[1])

    ref_out[...] = (own_ref + ref_halo[1].astype(F32)).astype(BF16)
    ref_near[core * 4 + y] = ref_out[...]

    @pl.loop(1, 8)
    def _(d):
        near_copy(d).start()

    def gather_far():
        bytes_of(ref_near.at[pl.ds(0, 7)], ref_sem.at[3])
        for c in range(2):
            packed = jnp.zeros((LOCAL, 128), F32)
            for group in range(4):
                packed = packed + jnp.where(
                    lane // 32 == group, ref_near[c * 4 + group].astype(F32), 0.0
                )
            ref_pack[c * LOCAL : (c + 1) * LOCAL, :] = packed.astype(BF16)
        ref_in[pl.ds(pl.multiple_of(z * 2 * LOCAL, 2 * LOCAL), 2 * LOCAL), :] = ref_pack[...]

        @pl.loop(1, 4)
        def _(d):
            far_copy(d).start()

    def turn(step):
        m = lax.rem(t // 2 + TILES - 1 - step, TILES)
        blocks = []
        for b in range(2):
            block = 2 * m + b

            @pl.when(block != t)
            def _():
                bytes_of(own_in.at[block], own_rs.at[block])

            @pl.when((block != 0) & (block != t + 1))
            def _():
                bytes_of(spill_in.at[block], spill_rs.at[block])

            own = own_in[block].astype(F32)
            head = own[0:SPILL_ROWS] + spill_in[block].astype(F32)
            own = jnp.concatenate([head, own[SPILL_ROWS:]], axis=0).astype(BF16).astype(F32)
            blocks += [own[f * LOCAL : (f + 1) * LOCAL] for f in range(FRAMES)]
        for to, block in enumerate(butterfly(blocks, lane)):
            send1[m, to * LOCAL : (to + 1) * LOCAL, :] = block.astype(BF16)
        mine = pl.ds(pl.multiple_of(s * LOCAL, LOCAL), LOCAL)
        v[m, mine, :] = send1[m, mine, :]

        for away in (2, 1, 3, 0):
            @pl.loop(0 if away else 1, 8)
            def _(d):
                near = lax.rem(y * 2 + core + d, 8)
                to = near // 2 * 8 + lax.rem(z + away, 4) * 2 + lax.rem(near, 2)
                turn_copy(m, to).start()

    def send_columns():
        bytes_of(ref_in.at[pl.ds(0, 6 * LOCAL)], ref_sem.at[5])
        row16 = lax.broadcasted_iota(jnp.int32, (2 * K, 1), 0)
        wanted = jnp.zeros((2 * K, 1), jnp.int32)
        for k in range(K):
            wanted = jnp.where(lax.rem(row16, K) == k, basis_in[k], wanted)
        column = lax.broadcasted_iota(jnp.int32, (2 * K, 128), 1)
        onehot = jnp.where(column == lax.rem(wanted, 128), 1.0, 0.0).astype(BF16)
        block = ref_in[...]
        picked = jnp.dot(onehot, block, preferred_element_type=F32)
        picked = jnp.where(lane // 32 == wanted // 128, picked, 0.0)
        picked = picked + pltpu.roll(picked, 64, 1)
        picked = picked + pltpu.roll(picked, 32, 1)
        swapped = jnp.where((lane & 1) == 0, -pltpu.roll(picked, 127, 1), pltpu.roll(picked, 1, 1))
        left = jnp.where(row16 < K, picked, swapped)
        parts = []
        for group in range(4):
            own = jnp.where(lane // 32 == group, left, 0.0).astype(BF16)
            parts.append(
                lax.dot_general(own, block, (((1,), (1,)), ((), ())), preferred_element_type=F32)
            )
        columns = jnp.concatenate(parts, axis=1).astype(BF16)
        cols_out[...] = columns
        cols_in[t] = columns

        @pl.loop(1, TM)
        def _(d):
            columns_copy(lax.rem(t + d, TM)).start()

    def find_basis():
        bytes_of(cols_in.at[pl.ds(0, TM - 1)], cols_sem.at[1])
        columns = cols_in[0].astype(F32)
        for other in range(1, TM):
            columns = columns + cols_in[other].astype(F32)
        columns = columns * (1.0 / SPECTRA)
        basis_re, basis_im = gram_schmidt(columns[0:K], columns[K:])
        basis[0:K, :] = basis_re
        basis[K:, :] = basis_im

    gather_far()
    for step in range(TILES):
        turn(step)
        if step == COLUMNS_AT:
            send_columns()
    find_basis()

    low = basis[...].astype(BF16)
    rows16 = lax.broadcasted_iota(jnp.int32, (16, 128), 0)
    lanes16 = lax.broadcasted_iota(jnp.int32, (16, 128), 1)
    keep = (lanes16 // 64 == rows16 // 8) & (lax.rem(lanes16, 4) == 2 * lax.rem(rows16, 8))
    spectrum = jnp.where(
        lax.rem(lax.broadcasted_iota(jnp.int32, (128, 128), 0) // 4, FRAMES)
        == lax.broadcasted_iota(jnp.int32, (128, 128), 1),
        1.0,
        0.0,
    )
    for step in range(TILES):
        m = lax.rem(t // 2 + TILES - 1 - step, TILES)
        bytes_of(v.at[m, pl.ds(0, INPUTS - LOCAL)], rs1.at[m])
        z = jnp.dot(low, v[m], preferred_element_type=F32)
        z_re = z[0:K] + pltpu.roll(z[K:], 127, 1)
        z_im = pltpu.roll(z[0:K], 127, 1) - z[K:]
        squares = jnp.sum(z_re * z_re + z_im * z_im, axis=0, keepdims=True)
        both = jnp.dot(
            jnp.where(keep, squares, 0.0), spectrum, precision=HIGHEST, preferred_element_type=F32
        )
        pow_out[2 * m] = both[0:8]
        pow_out[2 * m + 1] = both[8:16]
    pow_in[t] = pow_out[t]

    @pl.loop(1, TM)
    def _(d):
        power_copy(lax.rem(t + d, TM)).start()

    covariances(v, basis, cov, proj, lambda ch: None)

    bytes_of(pow_in.at[pl.ds(0, TM - 1)], pow_rs)
    for owner in range(TM):
        power[2 * owner : 2 * owner + 2, :] = pow_in[owner, 0:2, 0:FRAMES]

    bytes_of(cols_in.at[pl.ds(0, TM - 1)], cols_sem.at[0])
    bytes_of(ref_near.at[pl.ds(0, 7)], ref_sem.at[2])
    bytes_of(ref_in.at[pl.ds(0, 6 * LOCAL)], ref_sem.at[4])

    bytes_of(pow_out.at[pl.ds(0, TM - 1)], pow_ss)
    bytes_of(own_out.at[pl.ds(0, TM - 1)], own_ss)

    @pl.loop(0, TILES)
    def _(m):
        bytes_of(send1.at[m, pl.ds(0, INPUTS - LOCAL)], ss1.at[m])

    @pl.when(t < TM - 1)
    def _():
        bytes_of(ref_halo.at[0], ref_sem.at[0])
        bytes_of(spill_out.at[pl.ds(0, TM - 1)], spill_ss)


def channelise(volt, taps, table, ref_chan, basis_in):
    vmem = pl.BlockSpec(memory_space=pltpu.VMEM)
    hbm = pl.BlockSpec(memory_space=pltpu.HBM)
    dma = pltpu.SemaphoreType.DMA
    return pl.pallas_call(
        channelise_kernel,
        out_shape=(
            pltpu.VMEM((2, INPUTS, 2 * INPUTS), BF16),
            pltpu.VMEM((2, 2 * K * K), F32),
            pltpu.VMEM((16, FRAMES), F32),
        ),
        in_specs=[hbm] * 5,
        out_specs=(vmem, vmem, vmem),
        scratch_shapes=[
            pltpu.VMEM((VOLT_ROWS, 128), jnp.int32),
            pltpu.VMEM((TAPS, NFFT), F32),
            pltpu.SMEM((1,), jnp.int32),
            pltpu.SMEM((K,), jnp.int32),
            pltpu.VMEM((PIECES, 2 * NFFT, 256), BF16),
            pltpu.VMEM((TAPS * Q, 128), F32),
            pltpu.VMEM((FRAMES * LOCAL * Q, 128), F32),
            pltpu.VMEM((FRAMES * LOCAL, 2 * NFFT), BF16),
            pltpu.VMEM((TM, SPILL_ROWS, 128), BF16),
            pltpu.VMEM((TM, SPILL_ROWS, 128), BF16),
            pltpu.VMEM((TM, OWN_ROWS, 128), BF16),
            pltpu.VMEM((TM, OWN_ROWS, 128), BF16),
            pltpu.VMEM((TILES, INPUTS, 128), BF16),
            pltpu.VMEM((2 * K, INPUTS), F32),
            pltpu.VMEM((TILES, INPUTS, 128), BF16),
            pltpu.VMEM((2, LOCAL, 128), BF16),
            pltpu.VMEM((LOCAL, 128), BF16),
            pltpu.VMEM((8, LOCAL, 128), BF16),
            pltpu.VMEM((2 * LOCAL, 128), BF16),
            pltpu.VMEM((8 * LOCAL, 128), BF16),
            pltpu.VMEM((2 * K, INPUTS), BF16),
            pltpu.VMEM((TM, 2 * K, INPUTS), BF16),
            pltpu.VMEM((TM, 8, 128), F32),
            pltpu.VMEM((TM, 8, 128), F32),
            dma((PARTS,)),
            dma((3,)),
            dma,
            dma,
            dma((TM,)),
            dma,
            dma((TM,)),
            dma((TILES,)),
            dma((TILES,)),
            dma((6,)),
            dma((2,)),
            dma,
            dma,
        ],
        compiler_params=pltpu.CompilerParams(
            collective_id=0, has_side_effects=True, vmem_limit_bytes=LIMIT * 1024 * 1024
        ),
        name="channelise",
    )(volt, taps, table, ref_chan, basis_in)


def write_kernel(cov_in, proj_in, power_in, cov, proj, power, sem):
    def store(p):
        rows = pl.ds(p % 2 * (INPUTS // 2), INPUTS // 2)
        return pltpu.make_async_copy(cov_in.at[p // 2, rows], cov.at[p // 2, rows], sem.at[p])

    for p in range(4):
        store(p).start()
    proj[...] = proj_in[...]
    power[...] = power_in[...]
    for p in range(4):
        store(p).wait()


def write(cov, proj, power):
    vmem = pl.BlockSpec(memory_space=pltpu.VMEM)
    hbm = pl.BlockSpec(memory_space=pltpu.HBM)
    return pl.pallas_call(
        write_kernel,
        out_shape=tuple(jax.ShapeDtypeStruct(a.shape, a.dtype) for a in (cov, proj, power)),
        in_specs=[vmem, vmem, vmem],
        out_specs=(hbm, vmem, vmem),
        scratch_shapes=[pltpu.SemaphoreType.DMA((4,))],
        compiler_params=pltpu.CompilerParams(vmem_limit_bytes=16 * 1024 * 1024),
        name="write",
    )(cov, proj, power)


def on_device(table, voltages, filter_taps, reference_channel, basis_inputs):
    volt = voltages.reshape(LOCAL, 2, FRAMES * SUB, 128).transpose(0, 2, 1, 3).reshape(-1, 128)
    volt = pltpu.with_memory_space_constraint(volt, pltpu.HBM)
    table = pltpu.with_memory_space_constraint(table, pltpu.HBM)
    results = channelise(volt, filter_taps, table, reference_channel, basis_inputs)
    return write(*results)


def solution(mesh):
    table = transform_table()

    def whole(voltages, filter_taps, reference_channel, basis_inputs):
        return jax.shard_map(
            on_device,
            mesh=mesh,
            in_specs=(P(), P("stn", None, "tm"), P(), P(), P()),
            out_specs=(P(("stn", "tm"), None, None), P(("stn", "tm"), None), P("stn", "tm")),
            check_vma=False,
        )(jnp.asarray(table), voltages, filter_taps, reference_channel, basis_inputs)

    return whole
```
